512 devices in a mesh: rep: 16 (over z_hi, y), shard: 32 (over z_lo, x, core).
Axes of the slice: x: 4, y: 8, z: 8 (z_hi: 2, z_lo: 4; z = z_hi * 4 + z_lo), core: 2. Of those that a mesh axis runs over, the one named last changes fastest.
Arguments:
- activations: bfloat16 [65536, 8192], P('rep', 'shard'), may hold values from -6 to 6
- key_grads: bfloat16 [65536, 1024], P(('rep', 'shard')), may hold values from -0.09375 to 0.09375
- momentum: float32 [131072, 1024], P(('rep', 'shard')), may hold values from -6 to 6
- freq_rows: int32 [128, 16, 8], replicated, may hold values from 0 to 15, as said below
- freq_cols: int32 [128, 16, 8], replicated, may hold values from 0 to 15, as said below
- dispatch: int32 [32, 64], replicated, may hold values from 0 to 63, each once within a row
Outputs:
- new_momentum: float32 [131072, 1024], P(('rep', 'shard'))
- update: bfloat16 [2048, 4096], P('shard')
The draws below stay inside these ranges and needn't reach their ends.
Inputs may be any that keep to these rules, and one draw needn't show every extreme that they name: `freq_rows`: the 8 entries of one span are distinct. `freq_cols`: the 8 entries of one span are distinct. `dispatch`: each row names every number below 64 once.
All inputs are finite; a program needn't handle non-finite values.
Results may differ from the reference program's by a relative error of at most 0.001.
Values may be sent and summed in bfloat16 or wider, within the bound.
No kernel may reach another device: no remote copies, remote signals or barrier semaphores. Data moves between devices by JAX's collectives and lax.ppermute only.
A program may use at most 64 MiB of HBM per device.

```python
import jax
import jax.numpy as jnp
from jax import lax

D = 8192
KV = 1024
CH = 64
K = 8
BAND = 16
TOKG = 4096
CPD = 64
NCHUNK = 2048
N_REP = 16
N_SHARD = 32


def choose_band(key):
    scores = jax.random.randint(key, (D // CH, KV // CH, BAND), 0, 1 << 20) * BAND + jnp.arange(BAND, dtype=jnp.int32)
    ranking = jnp.argsort(scores, axis=-1, stable=True)
    return ranking[..., :K].astype(jnp.int32)


def draw_freq_rows(key, part):
    key = jax.random.fold_in(key, 11)
    return choose_band(key)


def draw_freq_cols(key, part):
    key = jax.random.fold_in(key, 23)
    return choose_band(key)


def level_of(own_key, extent, pieces, smallest, largest):
    def one(position, blocks):
        draws = jax.random.uniform(jax.random.fold_in(jax.random.fold_in(own_key, 6), position), (blocks,), jnp.float32, smallest / len(pieces), largest / len(pieces))
        return jnp.repeat(jnp.exp(draws), extent[position] // blocks).reshape((-1,) + (1,) * (len(extent) - position - 1))

    level = one(*pieces[0])
    for cut in pieces[1:]:
        level = level * one(*cut)
    return level


def gaussian(key, extent, width, limit, cuts=(), held_as=jnp.bfloat16):
    gain = level_of(key, extent, cuts, -0.22, 0.18) if cuts else 1.0
    entries = jax.random.normal(key, extent, jnp.float32) * width * gain
    return jnp.minimum(jnp.maximum(entries, -limit), limit).astype(held_as)


def setup_inputs(seed: int = 0) -> dict:
    key_list = jax.random.split(jax.random.key(seed), 7)
    return {
        "activations": gaussian(key_list[0], (N_REP * TOKG, D), 1.0, 6.0, ((0, 16), (1, 32))),
        "key_grads": gaussian(key_list[1], (N_REP * TOKG, KV), TOKG ** -0.5, 0.09375, ((0, 512),)),
        "momentum": gaussian(key_list[2], (N_REP * D, KV), 1.0, 6.0, ((0, 512),), jnp.float32),
        "freq_rows": draw_freq_rows(jax.random.fold_in(key_list[6], 71), 0),
        "freq_cols": draw_freq_cols(jax.random.fold_in(key_list[6], 71), 0),
        "dispatch": jax.vmap(lambda own: jax.random.permutation(own, CPD))(jax.random.split(key_list[5], N_SHARD)).reshape((N_SHARD, CPD)).astype(jnp.int32),
    }


def dct_table(size, dtype):
    frequency = jnp.arange(size, dtype=jnp.int32).astype(dtype)[:, None]
    sample = jnp.arange(size, dtype=jnp.int32).astype(dtype)[None, :]
    scales = jnp.where(frequency == 0, jnp.sqrt(1.0 / size), jnp.sqrt(2.0 / size)).astype(dtype)
    return scales * jnp.cos(jnp.pi * (2.0 * sample + 1.0) * frequency / (2.0 * size))

def basis_rows(indices, table):
    onehot = (indices[..., None] == jnp.arange(table.shape[0], dtype=jnp.int32)).astype(table.dtype)
    return jnp.einsum('...kf,fn->...kn', onehot, table, precision=lax.Precision.HIGHEST)

def encode(blocks, row_basis, col_basis):
    partial_rows = jnp.einsum('abin,anbm->abim', row_basis, blocks, precision=lax.Precision.HIGHEST)
    return jnp.einsum('abim,abjm->abij', partial_rows, col_basis, precision=lax.Precision.HIGHEST)

def decode_pairs(corner, row_basis, col_basis):
    partial_rows = jnp.einsum('abij,abin->abnj', corner, row_basis, precision=lax.Precision.HIGHEST)
    return jnp.einsum('abnj,abjm->abnm', partial_rows, col_basis, precision=lax.Precision.HIGHEST)

def reference(activations, key_grads, momentum, freq_rows, freq_cols, dispatch):
    row_count = D // CH
    col_count = KV // CH
    table = dct_table(CH, momentum.dtype)
    row_basis = basis_rows(freq_rows, table)
    col_basis = basis_rows(freq_cols, table)

    def group_step(group):
        inputs = lax.dynamic_slice_in_dim(activations, group * TOKG, TOKG, 0)
        outputs = lax.dynamic_slice_in_dim(key_grads, group * TOKG, TOKG, 0)
        grad = lax.dot_general(inputs, outputs, (((0,), (0,)), ((), ())), preferred_element_type=jnp.float32)
        moment = lax.dynamic_slice_in_dim(momentum, group * D, D, 0)
        fresh = 0.999 * moment + grad.astype(moment.dtype)
        blocks = fresh.reshape(row_count, CH, col_count, CH)
        corner = encode(blocks, row_basis, col_basis)
        local = decode_pairs(corner, row_basis, col_basis)
        local = jnp.transpose(local, (0, 2, 1, 3)).reshape(D, KV)
        return (fresh - local, corner)
    moments, corners = lax.map(group_step, jnp.arange(N_REP, dtype=jnp.int32))
    new_momentum = moments.reshape(N_REP * D, KV)
    total = lax.optimization_barrier(jnp.sum(corners, axis=0))
    dense = decode_pairs(total, row_basis, col_basis).reshape(NCHUNK, CH * CH)
    per_owner = CPD // N_SHARD
    slots = jnp.transpose(dispatch.reshape(N_SHARD, N_SHARD, per_owner), (1, 0, 2))
    span_ids = (jnp.arange(N_SHARD, dtype=jnp.int32)[None, :, None] * CPD + slots).reshape(-1)
    update = dense[span_ids].astype(jnp.bfloat16)
    return (new_momentum, update)
```

```python
import functools

import jax
import jax.numpy as jnp
import numpy as np
from jax import lax
from jax.experimental import pallas as pl
from jax.experimental.pallas import tpu as pltpu
from jax.sharding import PartitionSpec as P

CH = 64
K = 8
BAND = 16
ROWS = 256
WIDTH = 1024
F32 = jnp.float32
BF16 = jnp.bfloat16


def band_table():
    frequency = np.arange(BAND)[:, None]
    sample = np.arange(CH)[None, :]
    scales = np.where(frequency == 0, np.sqrt(1.0 / CH), np.sqrt(2.0 / CH))
    return scales * np.cos(np.pi * (2.0 * sample + 1.0) * frequency / (2.0 * CH))


def split_np(x):
    hi = x.astype(np.float32).astype(jnp.bfloat16)
    lo = (x - hi.astype(np.float64)).astype(np.float32).astype(jnp.bfloat16)
    return hi, lo


def block_basis():
    return np.kron(np.eye(4), band_table())


def pair_basis():
    return np.kron(band_table(), band_table())


def split(x):
    hi = x.astype(BF16)
    return hi, (x - hi.astype(F32)).astype(BF16)


def dot(x, y):
    return lax.dot_general(x, y, (((1,), (0,)), ((), ())), preferred_element_type=F32)


def dot3(x, y):
    (xh, xl), (yh, yl) = x, y
    return dot(xh, yh) + (dot(xh, yl) + dot(xl, yh))


def lanes(x, index):
    return jnp.take_along_axis(x, index, axis=1)


def encode_kernel(fresh, lh, ll, th, tl, mask, col_index, row_pick, slot_row, slot_lane, new, sent):
    left, right = (lh[...], ll[...]), (th[...], tl[...])
    whole = fresh[...]
    half = dot3(left, split(whole))
    parts = [dot3(split(half[:, q * 256:(q + 1) * 256]), right) for q in range(4)]
    low = jnp.concatenate(parts[:2], axis=1)
    high = jnp.concatenate(parts[2:], axis=1)

    lane = lax.broadcasted_iota(jnp.int32, (BAND, 128), 1)
    picked = []
    for a in range(4):
        rows = slice(a * BAND, (a + 1) * BAND)
        index = jnp.broadcast_to(col_index[a:a + 1, :], (BAND, 128))
        cols = jnp.where(lane < 64, lanes(low[rows], index), lanes(high[rows], index))
        want = row_pick[a * K:(a + 1) * K, :]
        total = jnp.zeros((K, 128), F32)
        for f in range(BAND):
            total = jnp.where(want == f, jnp.broadcast_to(cols[f:f + 1], (K, 128)), total)
        picked.append(total)
    code, place = slot_row[...], slot_lane[...]
    board = jnp.zeros((32, 128), F32)
    for a in range(4):
        for i in range(K):
            row = jnp.broadcast_to(picked[a][i:i + 1], (32, 128))
            board = jnp.where(code == a * K + i, lanes(row, place), board)
    sent[...] = board

    kept = [low * mask[:, :128], high * mask[:, 128:]]
    back = [dot3(right, split(part)) for part in kept]
    for q in range(4):
        piece = back[q // 2][:, (q % 2) * 64:(q % 2) * 64 + 64]
        cols = slice(q * 256, (q + 1) * 256)
        new[:, cols] = whole[:, cols] - dot3(split(piece), left)


def decode_kernel(received, index, kh, kl, out, first, second):
    total = received[0:32, :]
    for r in range(1, 16):
        total = total + received[r * 32:(r + 1) * 32, :]
    for k in range(2):
        for h in range(2):
            where = index[k * 32:(k + 1) * 32, h * 128:(h + 1) * 128]
            value = lanes(total, jnp.maximum(where, 0))
            spread = (first, second)[h]
            spread[pl.ds(k, 32, stride=2), :] = jnp.where(where >= 0, value, 0.0)
    pair = split(jnp.concatenate([first[...], second[...]], axis=1))
    for n in range(8):
        cols = slice(n * 512, (n + 1) * 512)
        out[:, cols] = dot3(pair, (kh[:, cols], kl[:, cols])).astype(BF16)


def vmem(n):
    return [pl.BlockSpec(memory_space=pltpu.VMEM)] * n


def encode(fresh, tables):
    lh, ll = split_np(block_basis())
    return pl.pallas_call(
        encode_kernel,
        out_shape=(jax.ShapeDtypeStruct((ROWS, WIDTH), F32), jax.ShapeDtypeStruct((32, 128), F32)),
        in_specs=vmem(10),
        out_specs=tuple(vmem(2)),
        compiler_params=pltpu.CompilerParams(vmem_limit_bytes=40 << 20),
        name="encode",
    )(fresh, lh, ll, lh.T.copy(), ll.T.copy(), *tables)


def decode(received, index):
    kh, kl = split_np(pair_basis())
    return pl.pallas_call(
        decode_kernel,
        out_shape=jax.ShapeDtypeStruct((64, CH * CH), BF16),
        in_specs=vmem(4),
        out_specs=pl.BlockSpec(memory_space=pltpu.VMEM),
        scratch_shapes=[pltpu.VMEM((64, 128), F32)] * 2,
        compiler_params=pltpu.CompilerParams(vmem_limit_bytes=40 << 20),
        name="decode",
    )(received, index, kh, kl)


def sender_tables(my_rows, my_cols, slots):
    band = jnp.arange(BAND, dtype=jnp.int32)
    in_rows = jnp.any(my_rows[..., None] == band, axis=2)
    in_cols = jnp.any(my_cols[..., None] == band, axis=2)
    mask = jnp.transpose(in_rows, (0, 2, 1))[..., None] & in_cols[:, None]
    mask = mask.reshape(4 * BAND, 16 * BAND).astype(F32)
    offset = (jnp.arange(16, dtype=jnp.int32) % 8 * BAND)[None, :, None]
    col_index = (my_cols + offset).reshape(4, 128)
    row_pick = jnp.broadcast_to(jnp.transpose(my_rows, (0, 2, 1))[..., None], (4, K, 16, K)).reshape(32, 128)
    order = slots.reshape(32, 2, 1, 1)
    i = jnp.arange(K, dtype=jnp.int32)
    slot_row = jnp.broadcast_to(order // 16 * K + i[:, None], (32, 2, K, K)).reshape(32, 128)
    slot_lane = jnp.broadcast_to(order % 16 * K + i, (32, 2, K, K)).reshape(32, 128)
    return mask, col_index, row_pick, slot_row, slot_lane


def owner_table(rows, cols):
    band = jnp.arange(BAND, dtype=jnp.int32)
    i = jnp.arange(K, dtype=jnp.int32)[:, None]

    def places(freq):
        hit = freq[..., None] == band
        return jnp.any(hit, axis=2), jnp.sum(jnp.where(hit, i, 0), axis=2)

    (row_in, row_at), (col_in, col_at) = places(rows), places(cols)
    start = (jnp.arange(2, dtype=jnp.int32) * 64)[None, :, None, None]
    index = start + row_at[..., None] * K + col_at[:, :, None]
    index = jnp.where(row_in[..., None] & col_in[:, :, None], index, -1)
    return jnp.transpose(index, (1, 0, 2, 3)).reshape(64, BAND * BAND)


def body(activations, key_grads, momentum, freq_rows, freq_cols, dispatch):
    position = lax.axis_index("shard")
    grad = lax.dot_general(
        activations,
        lax.all_gather(key_grads, "shard", axis=0, tiled=True),
        (((0,), (0,)), ((), ())),
        preferred_element_type=F32,
    )
    fresh = 0.999 * momentum + grad
    my_rows = lax.dynamic_slice_in_dim(freq_rows, position * 4, 4, 0)
    my_cols = lax.dynamic_slice_in_dim(freq_cols, position * 4, 4, 0)
    slots = lax.dynamic_slice_in_dim(dispatch, position, 1, 0).reshape(64)
    new_momentum, board = encode(fresh, sender_tables(my_rows, my_cols, slots))

    own = lax.dynamic_slice_in_dim(dispatch, position * 2, 2, 1)
    span_ids = (jnp.arange(32, dtype=jnp.int32)[:, None] * 64 + own).reshape(-1)
    own_rows = freq_rows.reshape(-1, K)[span_ids].reshape(32, 2, K)
    own_cols = freq_cols.reshape(-1, K)[span_ids].reshape(32, 2, K)
    index = owner_table(own_rows, own_cols)
    board = jnp.broadcast_to(board[None], (16, 32, 128)).reshape(512, 128)
    received = lax.all_to_all(board, ("rep", "shard"), 0, 0, tiled=True)
    update = decode(received, index)
    return (new_momentum, update)


def solution(mesh):
    in_specs = (
        P("rep", "shard"),
        P(("rep", "shard"), None),
        P(("rep", "shard"), None),
        P(),
        P(),
        P(),
    )
    out_specs = (P(("rep", "shard"), None), P("shard", None))
    return jax.shard_map(body, mesh=mesh, in_specs=in_specs, out_specs=out_specs, check_vma=False)
```

```python
import functools

import jax
import jax.numpy as jnp
import numpy as np
from jax import lax
from jax.experimental import pallas as pl
from jax.experimental.pallas import tpu as pltpu
from jax.sharding import PartitionSpec as P

CH = 64
K = 8
BAND = 16
ROWS = 256
WIDTH = 1024
SCALE = 2.0 ** 15
F32 = jnp.float32
BF16 = jnp.bfloat16


def band_table():
    frequency = np.arange(BAND)[:, None]
    sample = np.arange(CH)[None, :]
    scales = np.where(frequency == 0, np.sqrt(1.0 / CH), np.sqrt(2.0 / CH))
    return scales * np.cos(np.pi * (2.0 * sample + 1.0) * frequency / (2.0 * CH))


def split_np(x):
    hi = x.astype(np.float32).astype(jnp.bfloat16)
    lo = (x - hi.astype(np.float64)).astype(np.float32).astype(jnp.bfloat16)
    return hi, lo


def block_basis():
    return np.kron(np.eye(4), band_table())


def pair_basis():
    return np.kron(band_table(), band_table())


def split(x):
    hi = x.astype(BF16)
    return hi, (x - hi.astype(F32)).astype(BF16)


def dot(x, y):
    return lax.dot_general(x, y, (((1,), (0,)), ((), ())), preferred_element_type=F32)


def dot3(x, y):
    (xh, xl), (yh, yl) = x, y
    return dot(xh, yh) + (dot(xh, yl) + dot(xl, yh))


def lanes(x, index):
    return jnp.take_along_axis(x, index, axis=1)


def select(low, high, col_index, row_pick, slot_row, slot_lane):
    lane = lax.broadcasted_iota(jnp.int32, (BAND, 128), 1)
    picked = []
    for a in range(4):
        rows = slice(a * BAND, (a + 1) * BAND)
        index = jnp.broadcast_to(col_index[a:a + 1, :], (BAND, 128))
        cols = jnp.where(lane < 64, lanes(low[rows], index), lanes(high[rows], index))
        want = row_pick[a * K:(a + 1) * K, :]
        total = jnp.zeros((K, 128), F32)
        for f in range(BAND):
            total = jnp.where(want == f, jnp.broadcast_to(cols[f:f + 1], (K, 128)), total)
        picked.append(total)
    code, place = slot_row[...], slot_lane[...]
    board = jnp.zeros((32, 128), F32)
    for a in range(4):
        for i in range(K):
            row = jnp.broadcast_to(picked[a][i:i + 1], (32, 128))
            board = jnp.where(code == a * K + i, lanes(row, place), board)
    return board


def project_kernel(grads, th, tl, out):
    for q in range(4):
        part = grads[:, q * 256:(q + 1) * 256]
        out[:, q * 64:(q + 1) * 64] = (dot(part, th[...]) + dot(part, tl[...])) * SCALE


def nt(x, y):
    return lax.dot_general(x, y, (((1,), (1,)), ((), ())), preferred_element_type=F32)


def inputs_kernel(inputs, lh, ll, high, low):
    left = jnp.concatenate([lh[...], ll[...]], axis=0)
    for z in range(4):
        for x in range(4):
            for c in range(2):
                at = ((z * 4 + x) * 2 + c) * 128
                both = nt(left, inputs[at:at + 128, :])
                part = split(both[:64] + both[64:])
                to = (x * 4 + z) * 128
                high[c, :, to:to + 128] = part[0]
                low[c, :, to:to + 128] = part[1]


def moment_kernel(momentum, lh, ll, th, tl, out):
    left, right = (lh[...], ll[...]), (th[...], tl[...])
    half = dot3(left, split(0.999 * momentum[...]))
    for q in range(4):
        out[:, q * 64:(q + 1) * 64] = dot3(split(half[:, q * 256:(q + 1) * 256]), right)


def contract(high, low, side, source):
    xh, xl = split(source)
    both = dot(jnp.concatenate([high[side], low[side]], axis=0), xh)
    return (both[:64] + (both[64:] + dot(high[side], xl))) * (1.0 / SCALE)


def near_kernel(core, high, low, own, kept, out):
    out[...] = kept[...] + contract(high, low, core[0], own[...])


def far_kernel(core, high, low, other, near, col_index, row_pick, slot_row, slot_lane, coef, sent):
    total = near[...] + contract(high, low, 1 - core[0], other[...])
    coef[...] = total
    board = select(total[:, :128], total[:, 128:], col_index, row_pick, slot_row, slot_lane)
    for r in range(16):
        sent[r * 32:(r + 1) * 32, :] = board


def turn_kernel(inputs, out):
    for t in range(8):
        out[:, t * 512:(t + 1) * 512] = inputs[t * 512:(t + 1) * 512, :].T


def final_kernel(turned, grads, base, out):
    step = pl.program_id(0)

    @pl.when(step == 0)
    def _():
        out[...] = base[...]

    out[...] += dot(turned[...], grads[...])


def base_kernel(momentum, coef, mask, lh, ll, th, tl, out):
    left, right = (lh[...], ll[...]), (th[...], tl[...])
    back = dot3(right, split(coef[...] * mask[...]))
    for q in range(4):
        cols = slice(q * 256, (q + 1) * 256)
        out[:, cols] = 0.999 * momentum[:, cols] - dot3(split(back[:, q * 64:(q + 1) * 64]), left)


def decode_kernel(received, index, kh, kl, out, first, second):
    total = received[0:32, :]
    for r in range(1, 16):
        total = total + received[r * 32:(r + 1) * 32, :]
    for k in range(2):
        for h in range(2):
            where = index[k * 32:(k + 1) * 32, h * 128:(h + 1) * 128]
            value = lanes(total, jnp.maximum(where, 0))
            spread = (first, second)[h]
            spread[pl.ds(k, 32, stride=2), :] = jnp.where(where >= 0, value, 0.0)
    pair = split(jnp.concatenate([first[...], second[...]], axis=1))
    for n in range(8):
        cols = slice(n * 512, (n + 1) * 512)
        out[:, cols] = dot3(pair, (kh[:, cols], kl[:, cols])).astype(BF16)


def vmem(n):
    return [pl.BlockSpec(memory_space=pltpu.VMEM)] * n


def call(kernel, shapes, *args, scalars=0):
    scalar = [pl.BlockSpec(memory_space=pltpu.SMEM)] * scalars
    many = isinstance(shapes, tuple)
    return pl.pallas_call(
        kernel,
        out_shape=shapes,
        in_specs=scalar + vmem(len(args) - scalars),
        out_specs=tuple(vmem(len(shapes))) if many else vmem(1)[0],
        compiler_params=pltpu.CompilerParams(vmem_limit_bytes=40 << 20),
        name=kernel.__name__,
    )(*args)


def sds(shape, dtype=F32):
    return jax.ShapeDtypeStruct(shape, dtype)


def decode(received, index):
    kh, kl = split_np(pair_basis())
    return pl.pallas_call(
        decode_kernel,
        out_shape=jax.ShapeDtypeStruct((64, CH * CH), BF16),
        in_specs=vmem(4),
        out_specs=pl.BlockSpec(memory_space=pltpu.VMEM),
        scratch_shapes=[pltpu.VMEM((64, 128), F32)] * 2,
        compiler_params=pltpu.CompilerParams(vmem_limit_bytes=40 << 20),
        name="decode",
    )(received, index, kh, kl)


def sender_tables(my_rows, my_cols, slots):
    band = jnp.arange(BAND, dtype=jnp.int32)
    in_rows = jnp.any(my_rows[..., None] == band, axis=2)
    in_cols = jnp.any(my_cols[..., None] == band, axis=2)
    mask = jnp.transpose(in_rows, (0, 2, 1))[..., None] & in_cols[:, None]
    mask = mask.reshape(4 * BAND, 16 * BAND).astype(F32)
    offset = (jnp.arange(16, dtype=jnp.int32) % 8 * BAND)[None, :, None]
    col_index = (my_cols + offset).reshape(4, 128)
    row_pick = jnp.broadcast_to(jnp.transpose(my_rows, (0, 2, 1))[..., None], (4, K, 16, K)).reshape(32, 128)
    order = slots.reshape(32, 2, 1, 1)
    i = jnp.arange(K, dtype=jnp.int32)
    slot_row = jnp.broadcast_to(order // 16 * K + i[:, None], (32, 2, K, K)).reshape(32, 128)
    slot_lane = jnp.broadcast_to(order % 16 * K + i, (32, 2, K, K)).reshape(32, 128)
    return mask, col_index, row_pick, slot_row, slot_lane


def owner_table(rows, cols):
    band = jnp.arange(BAND, dtype=jnp.int32)
    i = jnp.arange(K, dtype=jnp.int32)[:, None]

    def places(freq):
        hit = freq[..., None] == band
        return jnp.any(hit, axis=2), jnp.sum(jnp.where(hit, i, 0), axis=2)

    (row_in, row_at), (col_in, col_at) = places(rows), places(cols)
    start = (jnp.arange(2, dtype=jnp.int32) * 64)[None, :, None, None]
    index = start + row_at[..., None] * K + col_at[:, :, None]
    index = jnp.where(row_in[..., None] & col_in[:, :, None], index, -1)
    return jnp.transpose(index, (1, 0, 2, 3)).reshape(64, BAND * BAND)


def shard(z, x, c):
    return (z * 4 + x) * 2 + c


ALONG_X = [[shard(z, x, c) for x in range(4)] for z in range(4) for c in range(2)]
ALONG_Z = [[shard(z, x, c) for z in range(4)] for x in range(4) for c in range(2)]
OTHER_CORE = [(i, i ^ 1) for i in range(32)]


def gather(block, groups):
    copies = jnp.broadcast_to(block[None], (4,) + block.shape).reshape((4 * block.shape[0],) + block.shape[1:])
    return lax.all_to_all(copies, "shard", 0, 0, tiled=True, axis_index_groups=groups)


def body(activations, key_grads, momentum, freq_rows, freq_cols, dispatch):
    position = lax.axis_index("shard")
    lh, ll = split_np(block_basis())
    th, tl = lh.T.copy(), ll.T.copy()
    all_grads = lax.all_gather(key_grads, "shard", axis=0, tiled=True)

    band = call(project_kernel, sds((128, 256)), key_grads, th, tl).astype(jnp.float16)
    along_z = gather(band, ALONG_Z)

    my_rows = lax.dynamic_slice_in_dim(freq_rows, position * 4, 4, 0)
    my_cols = lax.dynamic_slice_in_dim(freq_cols, position * 4, 4, 0)
    slots = lax.dynamic_slice_in_dim(dispatch, position, 1, 0).reshape(64)
    tables = sender_tables(my_rows, my_cols, slots)
    kept = call(moment_kernel, sds((64, 256)), momentum, lh, ll, th, tl)
    along_z, kept, (mask, *picks) = lax.optimization_barrier((along_z, kept, tables))
    own = gather(along_z, ALONG_X)

    high, low = call(inputs_kernel, (sds((2, 64, 2048), BF16),) * 2, activations, lh, ll)
    own_slots = lax.dynamic_slice_in_dim(dispatch, position * 2, 2, 1)
    span_ids = (jnp.arange(32, dtype=jnp.int32)[:, None] * 64 + own_slots).reshape(-1)
    own_rows = freq_rows.reshape(-1, K)[span_ids].reshape(32, 2, K)
    own_cols = freq_cols.reshape(-1, K)[span_ids].reshape(32, 2, K)
    index = owner_table(own_rows, own_cols)
    own, high, low, index = lax.optimization_barrier((own, high, low, index))

    other = lax.ppermute(own, "shard", OTHER_CORE)
    core = (position % 2).astype(jnp.int32).reshape(1)
    near = call(near_kernel, sds((64, 256)), core, high, low, own.astype(F32), kept, scalars=1)
    coef, board = call(
        far_kernel, (sds((64, 256)), sds((512, 128))),
        core, high, low, other.astype(F32), near, *picks, scalars=1,
    )
    received = lax.all_to_all(board, ("rep", "shard"), 0, 0, tiled=True)
    base = call(base_kernel, sds((ROWS, WIDTH)), momentum, coef, mask, lh, ll, th, tl)
    turned = call(turn_kernel, sds((ROWS, 4096), BF16), activations)
    received, base, turned = lax.optimization_barrier((received, base, turned))
    update = decode(received, index)

    new_momentum = pl.pallas_call(
        final_kernel,
        grid=(8,),
        out_shape=sds((ROWS, WIDTH)),
        in_specs=[
            pl.BlockSpec((ROWS, 512), lambda t: (0, t)),
            pl.BlockSpec((512, WIDTH), lambda t: (t, 0)),
            pl.BlockSpec((ROWS, WIDTH), lambda t: (0, 0)),
        ],
        out_specs=pl.BlockSpec((ROWS, WIDTH), lambda t: (0, 0)),
        compiler_params=pltpu.CompilerParams(vmem_limit_bytes=40 << 20),
        cost_estimate=pl.CostEstimate(flops=2 * 4096 * ROWS * WIDTH, bytes_accessed=14 << 20, transcendentals=0),
        name="final",
    )(turned, all_grads, base)
    return (new_momentum, update)


def solution(mesh):
    in_specs = (
        P("rep", "shard"),
        P(("rep", "shard"), None),
        P(("rep", "shard"), None),
        P(),
        P(),
        P(),
    )
    out_specs = (P(("rep", "shard"), None), P("shard", None))
    return jax.shard_map(body, mesh=mesh, in_specs=in_specs, out_specs=out_specs, check_vma=False)
```

```python
import jax
import jax.numpy as jnp
import numpy as np
from jax import lax
from jax.experimental import pallas as pl
from jax.experimental.pallas import tpu as pltpu
from jax.sharding import PartitionSpec as P

CH = 64
K = 8
BAND = 16
ROWS = 256
WIDTH = 1024
TOKENS = 4096
LEVELS = 32000.0
SENT = 144
F32 = jnp.float32
BF16 = jnp.bfloat16
I32 = jnp.int32


def band_table():
    frequency = np.arange(BAND)[:, None]
    sample = np.arange(CH)[None, :]
    scales = np.where(frequency == 0, np.sqrt(1.0 / CH), np.sqrt(2.0 / CH))
    return scales * np.cos(np.pi * (2.0 * sample + 1.0) * frequency / (2.0 * CH))


def split_np(x):
    hi = x.astype(np.float32).astype(jnp.bfloat16)
    lo = (x - hi.astype(np.float64)).astype(np.float32).astype(jnp.bfloat16)
    return hi, lo


def block_basis():
    return np.kron(np.eye(4), band_table())


def pair_basis():
    return np.kron(band_table(), band_table())


def split(x):
    hi = x.astype(BF16)
    return hi, (x - hi.astype(F32)).astype(BF16)


def dot(x, y):
    return lax.dot_general(x, y, (((1,), (0,)), ((), ())), preferred_element_type=F32)


def nt(x, y):
    return lax.dot_general(x, y, (((1,), (1,)), ((), ())), preferred_element_type=F32)


def dot3(x, y):
    (xh, xl), (yh, yl) = x, y
    return dot(xh, yh) + (dot(xh, yl) + dot(xl, yh))


def lanes(x, index):
    return jnp.take_along_axis(x, index, axis=1)


def iota(shape, axis):
    return lax.broadcasted_iota(I32, shape, axis)


def power(exponent):
    return jnp.exp2(exponent).astype(BF16).astype(F32)


def project_kernel(grads, th, tl, out):
    parts = []
    for q in range(4):
        part = grads[:, q * 256:(q + 1) * 256]
        parts.append(dot(part, th[...]) + dot(part, tl[...]))
    band = jnp.concatenate(parts, axis=1)
    top = jnp.maximum(jnp.max(jnp.abs(band), axis=1, keepdims=True), 1e-35)
    exponent = jnp.broadcast_to(jnp.ceil(jnp.log2(top)), (128, 128))
    code = jnp.floor(band * (power(-exponent[:, :1]) * LEVELS) + 0.5)
    scales = jnp.concatenate([exponent.T[:16]] * 2, axis=1)
    sent = jnp.concatenate([code, scales], axis=0).astype(I32).astype(jnp.int16)
    for k in range(4):
        out[k * SENT:(k + 1) * SENT, :] = sent


def tables_kernel(place, freq_rows, freq_cols, dispatch, mask, col_index, row_pick, slot_row, slot_lane, index):
    s = place[0]
    rows = freq_rows[...].reshape(128, 128).astype(F32).astype(BF16)
    cols = freq_cols[...].reshape(128, 128).astype(F32).astype(BF16)
    sub, lane = iota((8, 128), 0), iota((8, 128), 1)
    pick = jnp.where((lane == s * 4 + sub) & (sub < 4), 1.0, 0.0).astype(BF16)
    my_rows = nt(pick, rows).astype(I32)
    my_cols = nt(pick, cols).astype(I32)
    col_index[...] = my_cols + ((lane >> 3) & 7) * BAND
    for i in range(K):
        value = lanes(my_rows, (lane & 120) + i)
        for a in range(4):
            row_pick[a * K + i:a * K + i + 1, :] = value[a:a + 1]
    f1 = iota((BAND, 128), 0)
    for h in range(2):
        source = h * 64 + (lane >> 4) * K
        hit = jnp.zeros((8, 128), I32)
        for j in range(K):
            hit += jnp.where(lanes(my_cols, source + j) == (lane & 15), 1, 0)
        values = [lanes(my_rows, source + i) for i in range(K)]
        for a in range(4):
            found = jnp.zeros((BAND, 128), I32)
            for value in values:
                found += jnp.where(jnp.broadcast_to(value[a:a + 1], (BAND, 128)) == f1, 1, 0)
            both = found * jnp.broadcast_to(hit[a:a + 1], (BAND, 128))
            mask[a * BAND:(a + 1) * BAND, h * 128:(h + 1) * 128] = both.astype(F32)

    def doubled(x):
        return jnp.concatenate([x, x], axis=1)

    sub, lane = iota((32, 128), 0), iota((32, 128), 1)
    mine = jnp.broadcast_to(doubled(dispatch[pl.ds(s, 1), :]), (32, 128))
    slot = lanes(mine, sub * 2 + (lane >> 6))
    slot_row[...] = (slot >> 4) * K + ((lane >> 3) & 7)
    slot_lane[...] = (slot & 15) * K + (lane & 7)

    whole = doubled(dispatch[...])
    owned = [lanes(whole, jnp.zeros((32, 128), I32) + (s * 2 + k)) for k in range(2)]
    owned = jnp.concatenate(owned, axis=0)
    sub, lane = iota((64, 128), 0), iota((64, 128), 1)
    pick = jnp.where(lane == (sub & 31) * 4 + (owned >> 4), 1.0, 0.0).astype(BF16)
    own_rows = nt(pick, rows).astype(I32)
    own_cols = nt(pick, cols).astype(I32)
    first = (owned & 15) * K
    row_values = [lanes(own_rows, first + i) for i in range(K)]
    col_values = [lanes(own_cols, first + i) for i in range(K)]

    def at(values, frequency):
        seen, where = jnp.zeros((64, 128), I32), jnp.zeros((64, 128), I32)
        for i, value in enumerate(values):
            same = value == frequency
            seen += jnp.where(same, 1, 0)
            where += jnp.where(same, i, 0)
        return seen, where

    col_seen, col_at = at(col_values, lane & 15)
    start = (sub >> 5) * 64
    for h in range(2):
        row_seen, row_at = at(row_values, h * 8 + (lane >> 4))
        found = start + row_at * K + col_at
        index[:, h * 128:(h + 1) * 128] = jnp.where(row_seen * col_seen > 0, found, -1)


def prepare_kernel(inputs, momentum, lh, ll, th, tl, high, low, kept, turned):
    both_basis = jnp.concatenate([lh[...], ll[...]], axis=0)
    for z in range(4):
        for x in range(4):
            for c in range(2):
                at = ((z * 4 + x) * 2 + c) * 128
                block = inputs[at:at + 128, :]
                both = nt(both_basis, block)
                part = split(both[:64] + both[64:])
                to = (x * 4 + z) * 128
                high[c, :, to:to + 128] = part[0]
                low[c, :, to:to + 128] = part[1]
                turned[:, at:at + 128] = block.T
    left, right = (lh[...], ll[...]), (th[...], tl[...])
    half = dot3(left, split(0.999 * momentum[...]))
    for q in range(4):
        kept[:, q * 64:(q + 1) * 64] = dot3(split(half[:, q * 256:(q + 1) * 256]), right)


def contract(high, low, side, source):
    total = jnp.zeros((64, 256), F32)
    for k in range(16):
        at, to = k * SENT, k * 128
        xh, xl = split(source[at:at + 128, :].astype(I32).astype(F32))
        scale = power(source[at + 128:at + 144, :].astype(I32).astype(F32)[:1, :128]).astype(BF16)
        left = jnp.concatenate([high[side, :, to:to + 128], low[side, :, to:to + 128]], axis=0)
        left = left * jnp.broadcast_to(scale, (128, 128))
        both = dot(left, xh)
        total += both[:64] + (both[64:] + dot(left[:64], xl))
    return total * (1.0 / LEVELS)


def near_kernel(place, high, low, own, kept, out):
    out[...] = kept[...] + contract(high, low, place[0] & 1, own)


def select(low, high, col_index, row_pick, slot_row, slot_lane):
    lane = iota((BAND, 128), 1)
    picked = []
    for a in range(4):
        rows = slice(a * BAND, (a + 1) * BAND)
        index = jnp.broadcast_to(col_index[a:a + 1, :], (BAND, 128))
        cols = jnp.where(lane < 64, lanes(low[rows], index), lanes(high[rows], index))
        want = row_pick[a * K:(a + 1) * K, :]
        total = jnp.zeros((K, 128), F32)
        for f in range(BAND):
            total = jnp.where(want == f, jnp.broadcast_to(cols[f:f + 1], (K, 128)), total)
        picked.append(total)
    code, place = slot_row[...], slot_lane[...]
    board = jnp.zeros((32, 128), F32)
    for a in range(4):
        for i in range(K):
            row = jnp.broadcast_to(picked[a][i:i + 1], (32, 128))
            board = jnp.where(code == a * K + i, lanes(row, place), board)
    return board


def far_kernel(place, high, low, other, near, col_index, row_pick, slot_row, slot_lane, coef, sent):
    total = near[...] + contract(high, low, 1 - (place[0] & 1), other)
    coef[...] = total
    board = select(total[:, :128], total[:, 128:], col_index, row_pick, slot_row, slot_lane)
    for r in range(16):
        sent[r * 32:(r + 1) * 32, :] = board


def final_kernel(turned, grads, momentum, coef, mask, lh, ll, th, tl, out, done):
    @pl.when(pl.program_id(0) == 0)
    def _():
        left, right = (lh[...], ll[...]), (th[...], tl[...])
        back = dot3(right, split(coef[...] * mask[...]))
        for q in range(4):
            cols = slice(q * 256, (q + 1) * 256)
            out[:, cols] = 0.999 * momentum[:, cols] - dot3(split(back[:, q * 64:(q + 1) * 64]), left)
        done[...] = jnp.zeros((8, 128), F32)

    out[...] += dot(turned[...], grads[...])


def decode_kernel(received, index, kh, kl, done, out, first, second):
    @pl.when(pl.program_id(0) == 0)
    def _():
        total = received[0:32, :]
        for r in range(1, 16):
            total = total + received[r * 32:(r + 1) * 32, :]
        for k in range(2):
            for h in range(2):
                where = index[k * 32:(k + 1) * 32, h * 128:(h + 1) * 128]
                value = lanes(total, jnp.maximum(where, 0))
                spread = (first, second)[h]
                spread[pl.ds(k, 32, stride=2), :] = jnp.where(where >= 0, value, 0.0)

    pair = split(jnp.concatenate([first[...], second[...]], axis=1))
    out[...] = dot3(pair, (kh[...], kl[...])).astype(BF16)


def vmem(n):
    return [pl.BlockSpec(memory_space=pltpu.VMEM)] * n


def sds(shape, dtype=F32):
    return jax.ShapeDtypeStruct(shape, dtype)


def call(kernel, shapes, *args, scalars=0, limit=40):
    scalar = [pl.BlockSpec(memory_space=pltpu.SMEM)] * scalars
    many = isinstance(shapes, tuple)
    return pl.pallas_call(
        kernel,
        out_shape=shapes,
        in_specs=scalar + vmem(len(args) - scalars),
        out_specs=tuple(vmem(len(shapes))) if many else vmem(1)[0],
        compiler_params=pltpu.CompilerParams(vmem_limit_bytes=limit << 20),
        name=kernel.__name__,
    )(*args)


def whole(shape):
    return pl.BlockSpec(shape, lambda t: (0,) * len(shape))


def final(turned, grads, momentum, coef, mask, *basis):
    steps = 8
    size = TOKENS // steps
    return pl.pallas_call(
        final_kernel,
        grid=(steps,),
        out_shape=(sds((ROWS, WIDTH)), sds((8, 128))),
        in_specs=[
            pl.BlockSpec((ROWS, size), lambda t: (0, t)),
            pl.BlockSpec((size, WIDTH), lambda t: (t, 0)),
            whole((ROWS, WIDTH)), whole((64, 256)), whole((64, 256)),
            whole((64, 256)), whole((64, 256)), whole((256, 64)), whole((256, 64)),
        ],
        out_specs=(whole((ROWS, WIDTH)), whole((8, 128))),
        compiler_params=pltpu.CompilerParams(vmem_limit_bytes=56 << 20),
        cost_estimate=pl.CostEstimate(flops=2 * TOKENS * ROWS * WIDTH, bytes_accessed=14 << 20, transcendentals=0),
        name="final",
    )(turned, grads, momentum, coef, mask, *basis)


def decode(received, index, done):
    kh, kl = split_np(pair_basis())
    size = 1024
    return pl.pallas_call(
        decode_kernel,
        grid=(CH * CH // size,),
        out_shape=sds((64, CH * CH), BF16),
        in_specs=[
            whole((512, 128)), whole((64, 256)),
            pl.BlockSpec((256, size), lambda t: (0, t)), pl.BlockSpec((256, size), lambda t: (0, t)),
            pl.BlockSpec(memory_space=pl.ANY),
        ],
        out_specs=pl.BlockSpec((64, size), lambda t: (0, t)),
        scratch_shapes=[pltpu.VMEM((64, 128), F32)] * 2,
        compiler_params=pltpu.CompilerParams(vmem_limit_bytes=56 << 20),
        name="decode",
    )(received, index, kh, kl, done)


def shard(z, x, c):
    return (z * 4 + x) * 2 + c


ALONG_X = [[shard(z, x, c) for x in range(4)] for z in range(4) for c in range(2)]
ALONG_Z = [[shard(z, x, c) for z in range(4)] for x in range(4) for c in range(2)]
OTHER_CORE = [(i, i ^ 1) for i in range(32)]


def exchange(copies, groups):
    return lax.all_to_all(copies, "shard", 0, 0, tiled=True, axis_index_groups=groups)


def body(activations, key_grads, momentum, freq_rows, freq_cols, dispatch):
    place = lax.axis_index("shard").astype(I32).reshape(1)
    lh, ll = split_np(block_basis())
    th, tl = lh.T.copy(), ll.T.copy()
    all_grads = lax.all_gather(key_grads, "shard", axis=0, tiled=True)

    band = call(project_kernel, sds((4 * SENT, 256), jnp.int16), key_grads, th, tl)
    along_z = exchange(band, ALONG_Z)
    mask, col_index, row_pick, slot_row, slot_lane, index = call(
        tables_kernel,
        (sds((64, 256)), sds((8, 128), I32), sds((32, 128), I32), sds((32, 128), I32), sds((32, 128), I32),
         sds((64, 256), I32)),
        place, jnp.transpose(freq_rows, (1, 2, 0)), jnp.transpose(freq_cols, (1, 2, 0)), dispatch, scalars=1,
    )
    along_z, slot_row, after = lax.optimization_barrier((along_z, slot_row, jnp.asarray(lh)))
    own = exchange(jnp.broadcast_to(along_z[None], (4, 4 * SENT, 256)).reshape(16 * SENT, 256), ALONG_X)
    high, low, kept, turned = call(
        prepare_kernel,
        (sds((2, 64, 2048), BF16), sds((2, 64, 2048), BF16), sds((64, 256)), sds((ROWS, TOKENS), BF16)),
        activations, momentum, after, ll, th, tl,
    )
    own, kept = lax.optimization_barrier((own, kept))

    other = lax.ppermute(own, "shard", OTHER_CORE)
    near = call(near_kernel, sds((64, 256)), place, high, low, own, kept, scalars=1)
    coef, board = call(
        far_kernel, (sds((64, 256)), sds((512, 128))),
        place, high, low, other, near, col_index, row_pick, slot_row, slot_lane, scalars=1,
    )
    received = lax.all_to_all(board, ("rep", "shard"), 0, 0, tiled=True)
    new_momentum, done = final(turned, all_grads, momentum, coef, mask, lh, ll, th, tl)
    received, done = lax.optimization_barrier((received, done))
    update = decode(received, index, done)
    return (new_momentum, update)


def solution(mesh):
    in_specs = (
        P("rep", "shard"),
        P(("rep", "shard"), None),
        P(("rep", "shard"), None),
        P(),
        P(),
        P(),
    )
    out_specs = (P(("rep", "shard"), None), P("shard", None))
    return jax.shard_map(body, mesh=mesh, in_specs=in_specs, out_specs=out_specs, check_vma=False)
```

```python
import jax
import jax.numpy as jnp
import numpy as np
from jax import lax
from jax.experimental import pallas as pl
from jax.experimental.pallas import tpu as pltpu
from jax.sharding import PartitionSpec as P

CH = 64
K = 8
BAND = 16
ROWS = 256
WIDTH = 1024
TOKENS = 4096
STEPS = 8
LEVELS = 32000.0
SENT = 144
F32 = jnp.float32
BF16 = jnp.bfloat16
I32 = jnp.int32


def band_table():
    frequency = np.arange(BAND)[:, None]
    sample = np.arange(CH)[None, :]
    scales = np.where(frequency == 0, np.sqrt(1.0 / CH), np.sqrt(2.0 / CH))
    return scales * np.cos(np.pi * (2.0 * sample + 1.0) * frequency / (2.0 * CH))


def split_np(x):
    hi = x.astype(np.float32).astype(jnp.bfloat16)
    lo = (x - hi.astype(np.float64)).astype(np.float32).astype(jnp.bfloat16)
    return hi, lo


def block_basis():
    return np.kron(np.eye(4), band_table())


def split(x):
    hi = x.astype(BF16)
    return hi, (x - hi.astype(F32)).astype(BF16)


def dot(x, y):
    return lax.dot_general(x, y, (((1,), (0,)), ((), ())), preferred_element_type=F32)


def nt(x, y):
    return lax.dot_general(x, y, (((1,), (1,)), ((), ())), preferred_element_type=F32)


def dot3(x, y):
    (xh, xl), (yh, yl) = x, y
    return dot(xh, yh) + (dot(xh, yl) + dot(xl, yh))


def lanes(x, index):
    return jnp.take_along_axis(x, index, axis=1)


def iota(shape, axis):
    return lax.broadcasted_iota(I32, shape, axis)


def power(exponent):
    return jnp.exp2(exponent).astype(BF16).astype(F32)


def project_kernel(grads, th, tl, out):
    parts = []
    for q in range(4):
        part = grads[:, q * 256:(q + 1) * 256]
        parts.append(dot(part, th[...]) + dot(part, tl[...]))
    band = jnp.concatenate(parts, axis=1)
    top = jnp.maximum(jnp.max(jnp.abs(band), axis=1, keepdims=True), 1e-35)
    exponent = jnp.broadcast_to(jnp.ceil(jnp.log2(top)), (128, 128))
    code = jnp.floor(band * (power(-exponent[:, :1]) * LEVELS) + 0.5)
    scales = jnp.concatenate([exponent.T[:16]] * 2, axis=1)
    sent = jnp.concatenate([code, scales], axis=0).astype(I32).astype(jnp.int16)
    for k in range(4):
        out[k * SENT:(k + 1) * SENT, :] = sent


def tables_kernel(place, freq_rows, freq_cols, dispatch, mask, col_index, row_pick, slot_row, slot_lane, index):
    s = place[0]
    rows = freq_rows[...].reshape(128, 128).astype(F32).astype(BF16)
    cols = freq_cols[...].reshape(128, 128).astype(F32).astype(BF16)
    sub, lane = iota((8, 128), 0), iota((8, 128), 1)
    pick = jnp.where((lane == s * 4 + sub) & (sub < 4), 1.0, 0.0).astype(BF16)
    my_rows = nt(pick, rows).astype(I32)
    my_cols = nt(pick, cols).astype(I32)
    col_index[...] = my_cols + ((lane >> 3) & 7) * BAND
    for i in range(K):
        value = lanes(my_rows, (lane & 120) + i)
        for a in range(4):
            row_pick[a * K + i:a * K + i + 1, :] = value[a:a + 1]
    f1 = iota((BAND, 128), 0)
    for h in range(2):
        source = h * 64 + (lane >> 4) * K
        hit = jnp.zeros((8, 128), I32)
        for j in range(K):
            hit += jnp.where(lanes(my_cols, source + j) == (lane & 15), 1, 0)
        values = [lanes(my_rows, source + i) for i in range(K)]
        for a in range(4):
            found = jnp.zeros((BAND, 128), I32)
            for value in values:
                found += jnp.where(jnp.broadcast_to(value[a:a + 1], (BAND, 128)) == f1, 1, 0)
            both = found * jnp.broadcast_to(hit[a:a + 1], (BAND, 128))
            mask[a * BAND:(a + 1) * BAND, h * 128:(h + 1) * 128] = both.astype(F32)

    def doubled(x):
        return jnp.concatenate([x, x], axis=1)

    sub, lane = iota((32, 128), 0), iota((32, 128), 1)
    mine = jnp.broadcast_to(doubled(dispatch[pl.ds(s, 1), :]), (32, 128))
    slot = lanes(mine, sub * 2 + (lane >> 6))
    slot_row[...] = (slot >> 4) * K + ((lane >> 3) & 7)
    slot_lane[...] = (slot & 15) * K + (lane & 7)

    whole = doubled(dispatch[...])
    owned = [lanes(whole, jnp.zeros((32, 128), I32) + (s * 2 + k)) for k in range(2)]
    owned = jnp.concatenate(owned, axis=0)
    sub, lane = iota((64, 128), 0), iota((64, 128), 1)
    pick = jnp.where(lane == (sub & 31) * 4 + (owned >> 4), 1.0, 0.0).astype(BF16)
    own_rows = nt(pick, rows).astype(I32)
    own_cols = nt(pick, cols).astype(I32)
    first = (owned & 15) * K
    row_values = [lanes(own_rows, first + i) for i in range(K)]
    col_values = [lanes(own_cols, first + i) for i in range(K)]

    def at(values, frequency):
        seen, where = jnp.zeros((64, 128), I32), jnp.zeros((64, 128), I32)
        for i, value in enumerate(values):
            same = value == frequency
            seen += jnp.where(same, 1, 0)
            where += jnp.where(same, i, 0)
        return seen, where

    col_seen, col_at = at(col_values, lane & 15)
    start = (sub >> 5) * 64
    for h in range(2):
        row_seen, row_at = at(row_values, h * 8 + (lane >> 4))
        found = start + row_at * K + col_at
        index[:, h * 128:(h + 1) * 128] = jnp.where(row_seen * col_seen > 0, found, -1)


def prepare_kernel(inputs, momentum, lh, ll, th, tl, high, low, kept):
    both_basis = jnp.concatenate([lh[...], ll[...]], axis=0)
    for z in range(4):
        for x in range(4):
            for c in range(2):
                at = ((z * 4 + x) * 2 + c) * 128
                block = inputs[at:at + 128, :]
                both = nt(both_basis, block)
                part = split(both[:64] + both[64:])
                to = (x * 4 + z) * 128
                high[c, :, to:to + 128] = part[0]
                low[c, :, to:to + 128] = part[1]
    left, right = (lh[...], ll[...]), (th[...], tl[...])
    half = dot3(left, split(0.999 * momentum[...]))
    for q in range(4):
        kept[:, q * 64:(q + 1) * 64] = dot3(split(half[:, q * 256:(q + 1) * 256]), right)


def contract(high, low, side, source):
    total = jnp.zeros((64, 256), F32)
    for k in range(16):
        at, to = k * SENT, k * 128
        xh, xl = split(source[at:at + 128, :].astype(I32).astype(F32))
        scale = power(source[at + 128:at + 144, :].astype(I32).astype(F32)[:1, :128]).astype(BF16)
        left = jnp.concatenate([high[side, :, to:to + 128], low[side, :, to:to + 128]], axis=0)
        left = left * jnp.broadcast_to(scale, (128, 128))
        both = dot(left, xh)
        total += both[:64] + (both[64:] + dot(left[:64], xl))
    return total * (1.0 / LEVELS)


def near_kernel(place, high, low, own, kept, out):
    out[...] = kept[...] + contract(high, low, place[0] & 1, own)


def select(low, high, col_index, row_pick, slot_row, slot_lane):
    lane = iota((BAND, 128), 1)
    picked = []
    for a in range(4):
        rows = slice(a * BAND, (a + 1) * BAND)
        index = jnp.broadcast_to(col_index[a:a + 1, :], (BAND, 128))
        cols = jnp.where(lane < 64, lanes(low[rows], index), lanes(high[rows], index))
        want = row_pick[a * K:(a + 1) * K, :]
        total = jnp.zeros((K, 128), F32)
        for f in range(BAND):
            total = jnp.where(want == f, jnp.broadcast_to(cols[f:f + 1], (K, 128)), total)
        picked.append(total)
    code, place = slot_row[...], slot_lane[...]
    board = jnp.zeros((32, 128), F32)
    for a in range(4):
        for i in range(K):
            row = jnp.broadcast_to(picked[a][i:i + 1], (32, 128))
            board = jnp.where(code == a * K + i, lanes(row, place), board)
    return board


def far_kernel(place, high, low, other, near, col_index, row_pick, slot_row, slot_lane, coef, sent):
    total = near[...] + contract(high, low, 1 - (place[0] & 1), other)
    coef[...] = total
    board = select(total[:, :128], total[:, 128:], col_index, row_pick, slot_row, slot_lane)
    for r in range(16):
        sent[r * 32:(r + 1) * 32, :] = board


def ready_kernel(inputs, momentum, coef, mask, lh, ll, th, tl, turned, base):
    size = TOKENS // STEPS
    for k in range(STEPS):
        turned[k] = inputs[k * size:(k + 1) * size, :].T
    left, right = (lh[...], ll[...]), (th[...], tl[...])
    back = dot3(right, split(coef[...] * mask[...]))
    for q in range(4):
        cols = slice(q * 256, (q + 1) * 256)
        base[:, cols] = 0.999 * momentum[:, cols] - dot3(split(back[:, q * 64:(q + 1) * 64]), left)


def final_kernel(turned, grads, base, out, done, sides, held, start, sems):
    size = TOKENS // STEPS
    first = pltpu.make_async_copy(base, start, sems.at[2 * STEPS])
    copies = []
    for k in range(STEPS):
        rows = pl.ds(k * size, size)
        copies.append((
            pltpu.make_async_copy(turned.at[k], sides.at[k], sems.at[STEPS + k]),
            pltpu.make_async_copy(grads.at[rows], held.at[rows], sems.at[k]),
        ))
        for copy in copies[k]:
            copy.start()
        if k == 0:
            first.start()
    done[...] = jnp.zeros((8, 128), F32)
    for k in range(STEPS):
        for copy in copies[k]:
            copy.wait()
        if k == 0:
            first.wait()
        rows = slice(k * size, (k + 1) * size)
        for q in range(4):
            cols = slice(q * 256, (q + 1) * 256)
            out[:, cols] = (start if k == 0 else out)[:, cols] + dot(sides[k], held[rows, cols])


def decode_kernel(received, index, weights, lh, ll, done, out, first, second, wide):
    total = received[0:32, :]
    for r in range(1, 16):
        total = total + received[r * 32:(r + 1) * 32, :]
    for k in range(2):
        for h in range(2):
            where = index[k * 32:(k + 1) * 32, h * 128:(h + 1) * 128]
            value = lanes(total, jnp.maximum(where, 0))
            spread = (first, second)[h]
            spread[pl.ds(k, 32, stride=2), :] = jnp.where(where >= 0, value, 0.0)
    basis = (lh[...], ll[...])
    for q in range(4):
        part = (first, second)[q // 2][:, (q % 2) * 64:(q % 2) * 64 + 64]
        columns = dot3(split(part), basis)
        for f in range(4):
            piece = columns[:, f * 64:(f + 1) * 64]
            wide[q * 4 + f] = jnp.concatenate([piece, piece], axis=1)

    @pl.loop(0, CH // 2)
    def _(pair):
        row = pl.multiple_of(pair * BAND, BAND)
        factors = weights[pl.ds(row, BAND), :]
        value = wide[0] * factors[0:1]
        for f in range(1, BAND):
            value = value + wide[f] * factors[f:f + 1]
        out[:, pl.ds(pl.multiple_of(pair * 128, 128), 128)] = value.astype(BF16)


def vmem(n):
    return [pl.BlockSpec(memory_space=pltpu.VMEM)] * n


def sds(shape, dtype=F32):
    return jax.ShapeDtypeStruct(shape, dtype)


def call(kernel, shapes, *args, scalars=0, limit=40):
    scalar = [pl.BlockSpec(memory_space=pltpu.SMEM)] * scalars
    many = isinstance(shapes, tuple)
    return pl.pallas_call(
        kernel,
        out_shape=shapes,
        in_specs=scalar + vmem(len(args) - scalars),
        out_specs=tuple(vmem(len(shapes))) if many else vmem(1)[0],
        compiler_params=pltpu.CompilerParams(vmem_limit_bytes=limit << 20),
        name=kernel.__name__,
    )(*args)


def final(turned, grads, base):
    return pl.pallas_call(
        final_kernel,
        out_shape=(sds((ROWS, WIDTH)), sds((8, 128))),
        in_specs=[pl.BlockSpec(memory_space=pl.ANY)] * 3,
        out_specs=tuple(vmem(2)),
        scratch_shapes=[
            pltpu.VMEM((STEPS, ROWS, TOKENS // STEPS), BF16), pltpu.VMEM((TOKENS, WIDTH), BF16),
            pltpu.VMEM((ROWS, WIDTH), F32), pltpu.SemaphoreType.DMA((2 * STEPS + 1,)),
        ],
        compiler_params=pltpu.CompilerParams(vmem_limit_bytes=56 << 20),
        cost_estimate=pl.CostEstimate(flops=2 * TOKENS * ROWS * WIDTH, bytes_accessed=14 << 20, transcendentals=0),
        name="final",
    )(turned, grads, base)


def decode(received, index, lh, ll, done):
    table = band_table().T.reshape(CH // 2, 2, BAND).transpose(0, 2, 1)
    weights = np.repeat(table, 64, axis=2).reshape(CH // 2 * BAND, 128).astype(np.float32)
    return pl.pallas_call(
        decode_kernel,
        out_shape=sds((64, CH * CH), BF16),
        in_specs=vmem(5) + [pl.BlockSpec(memory_space=pl.ANY)],
        out_specs=vmem(1)[0],
        scratch_shapes=[pltpu.VMEM((64, 128), F32)] * 2 + [pltpu.VMEM((BAND, 64, 128), F32)],
        compiler_params=pltpu.CompilerParams(vmem_limit_bytes=24 << 20),
        name="decode",
    )(received, index, weights, lh, ll, done)


def shard(z, x, c):
    return (z * 4 + x) * 2 + c


ALONG_X = [[shard(z, x, c) for x in range(4)] for z in range(4) for c in range(2)]
ALONG_Z = [[shard(z, x, c) for z in range(4)] for x in range(4) for c in range(2)]
OTHER_CORE = [(i, i ^ 1) for i in range(32)]


def exchange(copies, groups):
    return lax.all_to_all(copies, "shard", 0, 0, tiled=True, axis_index_groups=groups)


def body(activations, key_grads, momentum, freq_rows, freq_cols, dispatch):
    place = lax.axis_index("shard").astype(I32).reshape(1)
    lh, ll = split_np(block_basis())
    th, tl = lh.T.copy(), ll.T.copy()
    all_grads = lax.all_gather(key_grads, "shard", axis=0, tiled=True)

    band = call(project_kernel, sds((4 * SENT, 256), jnp.int16), key_grads, th, tl, limit=56)
    along_z = exchange(band, ALONG_Z)
    mask, col_index, row_pick, slot_row, slot_lane, index = call(
        tables_kernel,
        (sds((64, 256)), sds((8, 128), I32), sds((32, 128), I32), sds((32, 128), I32), sds((32, 128), I32),
         sds((64, 256), I32)),
        place, jnp.transpose(freq_rows, (1, 2, 0)), jnp.transpose(freq_cols, (1, 2, 0)), dispatch, scalars=1,
    )
    along_z, slot_row, after = lax.optimization_barrier((along_z, slot_row, jnp.asarray(lh)))
    own = exchange(jnp.broadcast_to(along_z[None], (4, 4 * SENT, 256)).reshape(16 * SENT, 256), ALONG_X)
    high, low, kept = call(
        prepare_kernel,
        (sds((2, 64, 2048), BF16), sds((2, 64, 2048), BF16), sds((64, 256))),
        activations, momentum, after, ll, th, tl,
    )
    own, kept = lax.optimization_barrier((own, kept))

    other = lax.ppermute(own, "shard", OTHER_CORE)
    near = call(near_kernel, sds((64, 256)), place, high, low, own, kept, scalars=1)
    coef, board = call(
        far_kernel, (sds((64, 256)), sds((512, 128))),
        place, high, low, other, near, col_index, row_pick, slot_row, slot_lane, scalars=1,
    )
    received = lax.all_to_all(board, ("rep", "shard"), 0, 0, tiled=True)
    turned, base = call(
        ready_kernel, (sds((STEPS, ROWS, TOKENS // STEPS), BF16), sds((ROWS, WIDTH))),
        activations, momentum, coef, mask, lh, ll, th, tl,
    )
    new_momentum, done = final(turned, all_grads, base)
    received, done = lax.optimization_barrier((received, done))
    update = decode(received, index, lh, ll, done)
    return (new_momentum, update)


def solution(mesh):
    in_specs = (
        P("rep", "shard"),
        P(("rep", "shard"), None),
        P(("rep", "shard"), None),
        P(),
        P(),
        P(),
    )
    out_specs = (P(("rep", "shard"), None), P("shard", None))
    return jax.shard_map(body, mesh=mesh, in_specs=in_specs, out_specs=out_specs, check_vma=False)
```

```python
import jax
import jax.numpy as jnp
import numpy as np
from jax import lax
from jax.experimental import pallas as pl
from jax.experimental.pallas import tpu as pltpu
from jax.sharding import PartitionSpec as P

CH = 64
K = 8
BAND = 16
ROWS = 256
WIDTH = 1024
TOKENS = 4096
STEPS = 4
LEVELS = 32000.0
SENT = 144
F32 = jnp.float32
BF16 = jnp.bfloat16
I32 = jnp.int32


def band_table():
    frequency = np.arange(BAND)[:, None]
    sample = np.arange(CH)[None, :]
    scales = np.where(frequency == 0, np.sqrt(1.0 / CH), np.sqrt(2.0 / CH))
    return scales * np.cos(np.pi * (2.0 * sample + 1.0) * frequency / (2.0 * CH))


def split_np(x):
    hi = x.astype(np.float32).astype(jnp.bfloat16)
    lo = (x - hi.astype(np.float64)).astype(np.float32).astype(jnp.bfloat16)
    return hi, lo


def block_basis():
    return np.kron(np.eye(4), band_table())


def split(x):
    hi = x.astype(BF16)
    return hi, (x - hi.astype(F32)).astype(BF16)


def dot(x, y):
    return lax.dot_general(x, y, (((1,), (0,)), ((), ())), preferred_element_type=F32)


def nt(x, y):
    return lax.dot_general(x, y, (((1,), (1,)), ((), ())), preferred_element_type=F32)


def dot3(x, y):
    (xh, xl), (yh, yl) = x, y
    return dot(xh, yh) + (dot(xh, yl) + dot(xl, yh))


def lanes(x, index):
    return jnp.take_along_axis(x, index, axis=1)


def iota(shape, axis):
    return lax.broadcasted_iota(I32, shape, axis)


def power(exponent):
    return jnp.exp2(exponent).astype(BF16).astype(F32)


def project_kernel(grads, th, tl, out):
    parts = []
    for q in range(4):
        part = grads[:, q * 256:(q + 1) * 256]
        parts.append(dot(part, th[...]) + dot(part, tl[...]))
    band = jnp.concatenate(parts, axis=1)
    top = jnp.maximum(jnp.max(jnp.abs(band), axis=1, keepdims=True), 1e-35)
    exponent = jnp.broadcast_to(jnp.ceil(jnp.log2(top)), (128, 128))
    code = jnp.floor(band * (power(-exponent[:, :1]) * LEVELS) + 0.5)
    scales = jnp.concatenate([exponent.T[:16]] * 2, axis=1)
    sent = jnp.concatenate([code, scales], axis=0).astype(I32).astype(jnp.int16)
    for k in range(4):
        out[k * SENT:(k + 1) * SENT, :] = sent


def tables_kernel(place, freq_rows, freq_cols, dispatch, mask, col_index, row_pick, slot_row, slot_lane, index):
    s = place[0]
    rows = freq_rows[...].reshape(128, 128).astype(F32).astype(BF16)
    cols = freq_cols[...].reshape(128, 128).astype(F32).astype(BF16)
    sub, lane = iota((8, 128), 0), iota((8, 128), 1)
    pick = jnp.where((lane == s * 4 + sub) & (sub < 4), 1.0, 0.0).astype(BF16)
    my_rows = nt(pick, rows).astype(I32)
    my_cols = nt(pick, cols).astype(I32)
    col_index[...] = my_cols + ((lane >> 3) & 7) * BAND
    for i in range(K):
        value = lanes(my_rows, (lane & 120) + i)
        for a in range(4):
            row_pick[a * K + i:a * K + i + 1, :] = value[a:a + 1]
    f1 = iota((BAND, 128), 0)
    for h in range(2):
        source = h * 64 + (lane >> 4) * K
        hit = jnp.zeros((8, 128), I32)
        for j in range(K):
            hit += jnp.where(lanes(my_cols, source + j) == (lane & 15), 1, 0)
        values = [lanes(my_rows, source + i) for i in range(K)]
        for a in range(4):
            found = jnp.zeros((BAND, 128), I32)
            for value in values:
                found += jnp.where(jnp.broadcast_to(value[a:a + 1], (BAND, 128)) == f1, 1, 0)
            both = found * jnp.broadcast_to(hit[a:a + 1], (BAND, 128))
            mask[a * BAND:(a + 1) * BAND, h * 128:(h + 1) * 128] = both.astype(F32)

    def doubled(x):
        return jnp.concatenate([x, x], axis=1)

    sub, lane = iota((32, 128), 0), iota((32, 128), 1)
    mine = jnp.broadcast_to(doubled(dispatch[pl.ds(s, 1), :]), (32, 128))
    slot = lanes(mine, sub * 2 + (lane >> 6))
    slot_row[...] = (slot >> 4) * K + ((lane >> 3) & 7)
    slot_lane[...] = (slot & 15) * K + (lane & 7)

    whole = doubled(dispatch[...])
    owned = [lanes(whole, jnp.zeros((32, 128), I32) + (s * 2 + k)) for k in range(2)]
    owned = jnp.concatenate(owned, axis=0)
    sub, lane = iota((64, 128), 0), iota((64, 128), 1)
    pick = jnp.where(lane == (sub & 31) * 4 + (owned >> 4), 1.0, 0.0).astype(BF16)
    own_rows = nt(pick, rows).astype(I32)
    own_cols = nt(pick, cols).astype(I32)
    first = (owned & 15) * K
    row_values = [lanes(own_rows, first + i) for i in range(K)]
    col_values = [lanes(own_cols, first + i) for i in range(K)]

    def at(values, frequency):
        seen, where = jnp.zeros((64, 128), I32), jnp.zeros((64, 128), I32)
        for i, value in enumerate(values):
            same = value == frequency
            seen += jnp.where(same, 1, 0)
            where += jnp.where(same, i, 0)
        return seen, where

    col_seen, col_at = at(col_values, lane & 15)
    start = (sub >> 5) * 64
    for h in range(2):
        row_seen, row_at = at(row_values, h * 8 + (lane >> 4))
        found = start + row_at * K + col_at
        index[:, h * 128:(h + 1) * 128] = jnp.where(row_seen * col_seen > 0, found, -1)


def prepare_kernel(inputs, momentum, lh, ll, th, tl, high, low, kept):
    both_basis = jnp.concatenate([lh[...], ll[...]], axis=0)
    for z in range(4):
        for x in range(4):
            for c in range(2):
                at = ((z * 4 + x) * 2 + c) * 128
                block = inputs[at:at + 128, :]
                both = nt(both_basis, block)
                part = split(both[:64] + both[64:])
                to = (x * 4 + z) * 128
                high[c, :, to:to + 128] = part[0]
                low[c, :, to:to + 128] = part[1]
    left, right = (lh[...], ll[...]), (th[...], tl[...])
    half = dot3(left, split(0.999 * momentum[...]))
    for q in range(4):
        kept[:, q * 64:(q + 1) * 64] = dot3(split(half[:, q * 256:(q + 1) * 256]), right)


def contract(high, low, side, source):
    total = jnp.zeros((64, 256), F32)
    for k in range(16):
        at, to = k * SENT, k * 128
        xh, xl = split(source[at:at + 128, :].astype(I32).astype(F32))
        scale = power(source[at + 128:at + 144, :].astype(I32).astype(F32)[:1, :128]).astype(BF16)
        left = jnp.concatenate([high[side, :, to:to + 128], low[side, :, to:to + 128]], axis=0)
        left = left * jnp.broadcast_to(scale, (128, 128))
        both = dot(left, xh)
        total += both[:64] + (both[64:] + dot(left[:64], xl))
    return total * (1.0 / LEVELS)


def near_kernel(place, high, low, own, kept, out):
    out[...] = kept[...] + contract(high, low, place[0] & 1, own)


def select(low, high, col_index, row_pick, slot_row, slot_lane):
    lane = iota((BAND, 128), 1)
    picked = []
    for a in range(4):
        rows = slice(a * BAND, (a + 1) * BAND)
        index = jnp.broadcast_to(col_index[a:a + 1, :], (BAND, 128))
        cols = jnp.where(lane < 64, lanes(low[rows], index), lanes(high[rows], index))
        want = row_pick[a * K:(a + 1) * K, :]
        total = jnp.zeros((K, 128), F32)
        for f in range(BAND):
            total = jnp.where(want == f, jnp.broadcast_to(cols[f:f + 1], (K, 128)), total)
        picked.append(total)
    code, place = slot_row[...], slot_lane[...]
    board = jnp.zeros((32, 128), F32)
    for a in range(4):
        for i in range(K):
            row = jnp.broadcast_to(picked[a][i:i + 1], (32, 128))
            board = jnp.where(code == a * K + i, lanes(row, place), board)
    return board


def far_kernel(place, high, low, other, near, col_index, row_pick, slot_row, slot_lane, coef, sent):
    total = near[...] + contract(high, low, 1 - (place[0] & 1), other)
    coef[...] = total
    board = select(total[:, :128], total[:, 128:], col_index, row_pick, slot_row, slot_lane)
    for r in range(16):
        sent[r * 32:(r + 1) * 32, :] = board


def ready_kernel(inputs, momentum, coef, mask, lh, ll, th, tl, turned, base):
    size = TOKENS // STEPS
    for k in range(STEPS):
        turned[k] = inputs[k * size:(k + 1) * size, :].T
    left, right = (lh[...], ll[...]), (th[...], tl[...])
    back = dot3(right, split(coef[...] * mask[...]))
    for q in range(4):
        cols = slice(q * 256, (q + 1) * 256)
        base[:, cols] = 0.999 * momentum[:, cols] - dot3(split(back[:, q * 64:(q + 1) * 64]), left)


def final_kernel(turned, grads, base, *refs):
    sources, (out, update), (sides, held, start), refs = refs[:5], refs[5:7], refs[7:10], refs[10:]
    (received, index, weights, lh, ll), (first, second, wide, rows, sems) = refs[:5], refs[5:]
    size = TOKENS // STEPS
    last = 2 * STEPS
    small = [pltpu.make_async_copy(x, y, sems.at[last + 1 + k]) for k, (x, y) in enumerate(zip(sources, refs[:5]))]
    small.append(pltpu.make_async_copy(base, start, sems.at[last]))
    for copy in small:
        copy.start()
    copies = []
    for k in range(STEPS):
        part = pl.ds(k * size, size)
        copies.append((
            pltpu.make_async_copy(turned.at[k], sides.at[k], sems.at[STEPS + k]),
            pltpu.make_async_copy(grads.at[part], held.at[part], sems.at[k]),
        ))
        for copy in copies[k]:
            copy.start()

    for copy in small:
        copy.wait()
    total = received[0:32, :]
    for r in range(1, 16):
        total = total + received[r * 32:(r + 1) * 32, :]
    for k in range(2):
        for h in range(2):
            where = index[k * 32:(k + 1) * 32, h * 128:(h + 1) * 128]
            value = lanes(total, jnp.maximum(where, 0))
            spread = (first, second)[h]
            spread[pl.ds(k, 32, stride=2), :] = jnp.where(where >= 0, value, 0.0)
    basis = (lh[...], ll[...])
    for q in range(4):
        part = (first, second)[q // 2][:, (q % 2) * 64:(q % 2) * 64 + 64]
        columns = dot3(split(part), basis)
        for f in range(4):
            piece = columns[:, f * 64:(f + 1) * 64]
            wide[q * 4 + f] = jnp.concatenate([piece, piece], axis=1)

    @pl.loop(0, CH // 2, unroll=4)
    def _(pair):
        row = pl.multiple_of(pair * BAND, BAND)
        factors = weights[pl.ds(row, BAND), :]
        value = wide[0] * factors[0:1]
        for f in range(1, BAND):
            value = value + wide[f] * factors[f:f + 1]
        rows[:, pl.ds(pl.multiple_of(pair * 128, 128), 128)] = value.astype(BF16)

    decoded = pltpu.make_async_copy(rows, update, sems.at[last + 6])
    decoded.start()
    for k in range(STEPS):
        for copy in copies[k]:
            copy.wait()
        part = slice(k * size, (k + 1) * size)
        for q in range(4):
            cols = slice(q * 256, (q + 1) * 256)
            out[:, cols] = (start if k == 0 else out)[:, cols] + dot(sides[k], held[part, cols])
    decoded.wait()


def vmem(n):
    return [pl.BlockSpec(memory_space=pltpu.VMEM)] * n


def sds(shape, dtype=F32):
    return jax.ShapeDtypeStruct(shape, dtype)


def call(kernel, shapes, *args, scalars=0, limit=40):
    scalar = [pl.BlockSpec(memory_space=pltpu.SMEM)] * scalars
    many = isinstance(shapes, tuple)
    return pl.pallas_call(
        kernel,
        out_shape=shapes,
        in_specs=scalar + vmem(len(args) - scalars),
        out_specs=tuple(vmem(len(shapes))) if many else vmem(1)[0],
        compiler_params=pltpu.CompilerParams(vmem_limit_bytes=limit << 20),
        name=kernel.__name__,
    )(*args)


def final(turned, grads, base, received, index, lh, ll):
    table = band_table().T.reshape(CH // 2, 2, BAND).transpose(0, 2, 1)
    weights = np.repeat(table, 64, axis=2).reshape(CH // 2 * BAND, 128).astype(np.float32)
    return pl.pallas_call(
        final_kernel,
        out_shape=(sds((ROWS, WIDTH)), sds((64, CH * CH), BF16)),
        in_specs=[pl.BlockSpec(memory_space=pl.ANY)] * 8,
        out_specs=(vmem(1)[0], pl.BlockSpec(memory_space=pl.ANY)),
        scratch_shapes=[
            pltpu.VMEM((STEPS, ROWS, TOKENS // STEPS), BF16), pltpu.VMEM((TOKENS, WIDTH), BF16),
            pltpu.VMEM((ROWS, WIDTH), F32),
            pltpu.VMEM((512, 128), F32), pltpu.VMEM((64, 256), I32), pltpu.VMEM((CH // 2 * BAND, 128), F32),
            pltpu.VMEM((64, 256), BF16), pltpu.VMEM((64, 256), BF16),
            pltpu.VMEM((64, 128), F32), pltpu.VMEM((64, 128), F32), pltpu.VMEM((BAND, 64, 128), F32),
            pltpu.VMEM((64, CH * CH), BF16), pltpu.SemaphoreType.DMA((2 * STEPS + 7,)),
        ],
        compiler_params=pltpu.CompilerParams(vmem_limit_bytes=56 << 20),
        cost_estimate=pl.CostEstimate(flops=2 * TOKENS * ROWS * WIDTH, bytes_accessed=14 << 20, transcendentals=0),
        name="final",
    )(turned, grads, base, received, index, weights, lh, ll)


def shard(z, x, c):
    return (z * 4 + x) * 2 + c


ALONG_X = [[shard(z, x, c) for x in range(4)] for z in range(4) for c in range(2)]
ALONG_Z = [[shard(z, x, c) for z in range(4)] for x in range(4) for c in range(2)]
OTHER_CORE = [(i, i ^ 1) for i in range(32)]


def exchange(copies, groups):
    return lax.all_to_all(copies, "shard", 0, 0, tiled=True, axis_index_groups=groups)


def body(activations, key_grads, momentum, freq_rows, freq_cols, dispatch):
    place = lax.axis_index("shard").astype(I32).reshape(1)
    lh, ll = split_np(block_basis())
    th, tl = lh.T.copy(), ll.T.copy()
    all_grads = lax.all_gather(key_grads, "shard", axis=0, tiled=True)

    band = call(project_kernel, sds((4 * SENT, 256), jnp.int16), key_grads, th, tl, limit=56)
    along_z = exchange(band, ALONG_Z)
    mask, col_index, row_pick, slot_row, slot_lane, index = call(
        tables_kernel,
        (sds((64, 256)), sds((8, 128), I32), sds((32, 128), I32), sds((32, 128), I32), sds((32, 128), I32),
         sds((64, 256), I32)),
        place, jnp.transpose(freq_rows, (1, 2, 0)), jnp.transpose(freq_cols, (1, 2, 0)), dispatch, scalars=1,
    )
    along_z, slot_row, after = lax.optimization_barrier((along_z, slot_row, jnp.asarray(lh)))
    own = exchange(jnp.broadcast_to(along_z[None], (4, 4 * SENT, 256)).reshape(16 * SENT, 256), ALONG_X)
    high, low, kept = call(
        prepare_kernel,
        (sds((2, 64, 2048), BF16), sds((2, 64, 2048), BF16), sds((64, 256))),
        activations, momentum, after, ll, th, tl,
    )
    own, kept = lax.optimization_barrier((own, kept))

    other = lax.ppermute(own, "shard", OTHER_CORE)
    near = call(near_kernel, sds((64, 256)), place, high, low, own, kept, scalars=1)
    coef, board = call(
        far_kernel, (sds((64, 256)), sds((512, 128))),
        place, high, low, other, near, col_index, row_pick, slot_row, slot_lane, scalars=1,
    )
    received = lax.all_to_all(board, ("rep", "shard"), 0, 0, tiled=True)
    turned, base = call(
        ready_kernel, (sds((STEPS, ROWS, TOKENS // STEPS), BF16), sds((ROWS, WIDTH))),
        activations, momentum, coef, mask, lh, ll, th, tl,
    )
    new_momentum, update = final(turned, all_grads, base, received, index, lh, ll)
    return (new_momentum, update)


def solution(mesh):
    in_specs = (
        P("rep", "shard"),
        P(("rep", "shard"), None),
        P(("rep", "shard"), None),
        P(),
        P(),
        P(),
    )
    out_specs = (P(("rep", "shard"), None), P("shard", None))
    return jax.shard_map(body, mesh=mesh, in_specs=in_specs, out_specs=out_specs, check_vma=False)
```

```python
import jax
import jax.numpy as jnp
import numpy as np
from jax import lax
from jax.experimental import pallas as pl
from jax.experimental.pallas import tpu as pltpu
from jax.sharding import PartitionSpec as P

CH = 64
K = 8
BAND = 16
ROWS = 256
WIDTH = 1024
TOKENS = 4096
STEPS = 4
LEVELS = 32000.0
SENT = 144
PACKED = 528
F32 = jnp.float32
BF16 = jnp.bfloat16
I32 = jnp.int32


def band_table():
    frequency = np.arange(BAND)[:, None]
    sample = np.arange(CH)[None, :]
    scales = np.where(frequency == 0, np.sqrt(1.0 / CH), np.sqrt(2.0 / CH))
    return scales * np.cos(np.pi * (2.0 * sample + 1.0) * frequency / (2.0 * CH))


def split_np(x):
    hi = x.astype(np.float32).astype(jnp.bfloat16)
    lo = (x - hi.astype(np.float64)).astype(np.float32).astype(jnp.bfloat16)
    return hi, lo


def block_basis():
    return np.kron(np.eye(4), band_table())


def split(x):
    hi = x.astype(BF16)
    return hi, (x - hi.astype(F32)).astype(BF16)


def dot(x, y):
    return lax.dot_general(x, y, (((1,), (0,)), ((), ())), preferred_element_type=F32)


def nt(x, y):
    return lax.dot_general(x, y, (((1,), (1,)), ((), ())), preferred_element_type=F32)


def dot3(x, y):
    (xh, xl), (yh, yl) = x, y
    return dot(xh, yh) + (dot(xh, yl) + dot(xl, yh))


def lanes(x, index):
    return jnp.take_along_axis(x, index, axis=1)


def iota(shape, axis):
    return lax.broadcasted_iota(I32, shape, axis)


def power(exponent):
    return jnp.exp2(exponent).astype(BF16).astype(F32)


def project_kernel(grads, th, tl, out):
    parts = []
    for q in range(4):
        part = grads[:, q * 256:(q + 1) * 256]
        parts.append(dot(part, th[...]) + dot(part, tl[...]))
    band = jnp.concatenate(parts, axis=1)
    top = jnp.maximum(jnp.max(jnp.abs(band), axis=1, keepdims=True), 1e-35)
    exponent = jnp.broadcast_to(jnp.ceil(jnp.log2(top)), (128, 128))
    code = jnp.floor(band * (power(-exponent[:, :1]) * LEVELS) + 0.5)
    scales = jnp.concatenate([exponent.T[:16]] * 2, axis=1)
    sent = jnp.concatenate([code, scales], axis=0).astype(I32).astype(jnp.int16)
    for k in range(4):
        out[k * SENT:(k + 1) * SENT, :] = sent


def tables_kernel(place, freq_rows, freq_cols, dispatch, mask, col_index, row_pick, slot_row, slot_lane, index):
    s = place[0]
    rows = freq_rows[...].reshape(128, 128).astype(F32).astype(BF16)
    cols = freq_cols[...].reshape(128, 128).astype(F32).astype(BF16)
    sub, lane = iota((8, 128), 0), iota((8, 128), 1)
    pick = jnp.where((lane == s * 4 + sub) & (sub < 4), 1.0, 0.0).astype(BF16)
    my_rows = nt(pick, rows).astype(I32)
    my_cols = nt(pick, cols).astype(I32)
    col_index[...] = my_cols + ((lane >> 3) & 7) * BAND
    for i in range(K):
        value = lanes(my_rows, (lane & 120) + i)
        for a in range(4):
            row_pick[a * K + i:a * K + i + 1, :] = value[a:a + 1]
    f1 = iota((BAND, 128), 0)
    for h in range(2):
        source = h * 64 + (lane >> 4) * K
        hit = jnp.zeros((8, 128), I32)
        for j in range(K):
            hit += jnp.where(lanes(my_cols, source + j) == (lane & 15), 1, 0)
        values = [lanes(my_rows, source + i) for i in range(K)]
        for a in range(4):
            found = jnp.zeros((BAND, 128), I32)
            for value in values:
                found += jnp.where(jnp.broadcast_to(value[a:a + 1], (BAND, 128)) == f1, 1, 0)
            both = found * jnp.broadcast_to(hit[a:a + 1], (BAND, 128))
            mask[a * BAND:(a + 1) * BAND, h * 128:(h + 1) * 128] = both.astype(F32)

    def doubled(x):
        return jnp.concatenate([x, x], axis=1)

    sub, lane = iota((32, 128), 0), iota((32, 128), 1)
    mine = jnp.broadcast_to(doubled(dispatch[pl.ds(s, 1), :]), (32, 128))
    slot = lanes(mine, sub * 2 + (lane >> 6))
    slot_row[...] = (slot >> 4) * K + ((lane >> 3) & 7)
    slot_lane[...] = (slot & 15) * K + (lane & 7)

    whole = doubled(dispatch[...])
    owned = [lanes(whole, jnp.zeros((32, 128), I32) + (s * 2 + k)) for k in range(2)]
    owned = jnp.concatenate(owned, axis=0)
    sub, lane = iota((64, 128), 0), iota((64, 128), 1)
    pick = jnp.where(lane == (sub & 31) * 4 + (owned >> 4), 1.0, 0.0).astype(BF16)
    own_rows = nt(pick, rows).astype(I32)
    own_cols = nt(pick, cols).astype(I32)
    first = (owned & 15) * K
    row_values = [lanes(own_rows, first + i) for i in range(K)]
    col_values = [lanes(own_cols, first + i) for i in range(K)]

    def at(values, frequency):
        seen, where = jnp.zeros((64, 128), I32), jnp.zeros((64, 128), I32)
        for i, value in enumerate(values):
            same = value == frequency
            seen += jnp.where(same, 1, 0)
            where += jnp.where(same, i, 0)
        return seen, where

    col_seen, col_at = at(col_values, lane & 15)
    start = (sub >> 5) * 64
    for h in range(2):
        row_seen, row_at = at(row_values, h * 8 + (lane >> 4))
        found = start + row_at * K + col_at
        index[:, h * 128:(h + 1) * 128] = jnp.where(row_seen * col_seen > 0, found, -1)


def prepare_kernel(inputs, momentum, lh, ll, th, tl, high, low, kept):
    both_basis = jnp.concatenate([lh[...], ll[...]], axis=0)
    for z in range(4):
        for x in range(4):
            for c in range(2):
                at = ((z * 4 + x) * 2 + c) * 128
                block = inputs[at:at + 128, :]
                both = nt(both_basis, block)
                part = split(both[:64] + both[64:])
                to = (x * 4 + z) * 128
                high[c, :, to:to + 128] = part[0]
                low[c, :, to:to + 128] = part[1]
    left, right = (lh[...], ll[...]), (th[...], tl[...])
    half = dot3(left, split(0.999 * momentum[...]))
    for q in range(4):
        kept[:, q * 64:(q + 1) * 64] = dot3(split(half[:, q * 256:(q + 1) * 256]), right)


def repack_kernel(along_z, out):
    row = iota((16, 256), 0)
    scales = jnp.zeros((16, 256), I32)
    for z in range(4):
        scales = jnp.where(row == z, along_z[z * SENT + 128:(z + 1) * SENT, :].astype(I32), scales)
    scales = scales.astype(jnp.int16)
    for x in range(4):
        for z in range(4):
            out[x * PACKED + z * 128:x * PACKED + (z + 1) * 128, :] = along_z[z * SENT:z * SENT + 128, :]
        out[x * PACKED + 512:(x + 1) * PACKED, :] = scales


def contract(high, low, side, source):
    total = jnp.zeros((64, 256), F32)
    for k in range(16):
        x, z = k // 4, k % 4
        at, to = x * PACKED + z * 128, k * 128
        xh, xl = split(source[at:at + 128, :].astype(I32).astype(F32))
        scale = power(source[x * PACKED + 512:(x + 1) * PACKED, :].astype(I32).astype(F32)[z:z + 1, :128]).astype(BF16)
        left = jnp.concatenate([high[side, :, to:to + 128], low[side, :, to:to + 128]], axis=0)
        left = left * jnp.broadcast_to(scale, (128, 128))
        both = dot(left, xh)
        total += both[:64] + (both[64:] + dot(left[:64], xl))
    return total * (1.0 / LEVELS)


def near_kernel(place, high, low, own, kept, out):
    out[...] = kept[...] + contract(high, low, place[0] & 1, own)


def select(low, high, col_index, row_pick, slot_row, slot_lane):
    lane = iota((BAND, 128), 1)
    picked = []
    for a in range(4):
        rows = slice(a * BAND, (a + 1) * BAND)
        index = jnp.broadcast_to(col_index[a:a + 1, :], (BAND, 128))
        cols = jnp.where(lane < 64, lanes(low[rows], index), lanes(high[rows], index))
        want = row_pick[a * K:(a + 1) * K, :]
        total = jnp.zeros((K, 128), F32)
        for f in range(BAND):
            total = jnp.where(want == f, jnp.broadcast_to(cols[f:f + 1], (K, 128)), total)
        picked.append(total)
    code, place = slot_row[...], slot_lane[...]
    board = jnp.zeros((32, 128), F32)
    for a in range(4):
        for i in range(K):
            row = jnp.broadcast_to(picked[a][i:i + 1], (32, 128))
            board = jnp.where(code == a * K + i, lanes(row, place), board)
    return board


def far_kernel(place, high, low, other, near, col_index, row_pick, slot_row, slot_lane, coef, sent, held, sem):
    total = near[...] + contract(high, low, 1 - (place[0] & 1), other)
    held[...] = total
    copy = pltpu.make_async_copy(held, coef, sem.at[0])
    copy.start()
    board = select(total[:, :128], total[:, 128:], col_index, row_pick, slot_row, slot_lane)
    for r in range(16):
        sent[r * 32:(r + 1) * 32, :] = board
    copy.wait()


def ready_kernel(inputs, momentum, coef, mask, lh, ll, th, tl, turned, base):
    size = TOKENS // STEPS
    for k in range(STEPS):
        turned[k] = inputs[k * size:(k + 1) * size, :].T
    left, right = (lh[...], ll[...]), (th[...], tl[...])
    back = dot3(right, split(coef[...] * mask[...]))
    for q in range(4):
        cols = slice(q * 256, (q + 1) * 256)
        base[:, cols] = 0.999 * momentum[:, cols] - dot3(split(back[:, q * 64:(q + 1) * 64]), left)


def final_kernel(turned, grads, base, *refs):
    sources, (out, update), (sides, held, start), refs = refs[:5], refs[5:7], refs[7:10], refs[10:]
    (received, index, weights, lh, ll), (first, second, wide, rows, sems) = refs[:5], refs[5:]
    size = TOKENS // STEPS
    last = 2 * STEPS
    small = [pltpu.make_async_copy(x, y, sems.at[last + 1 + k]) for k, (x, y) in enumerate(zip(sources, refs[:5]))]
    small.append(pltpu.make_async_copy(base, start, sems.at[last]))
    for copy in small:
        copy.start()
    copies = []
    for k in range(STEPS):
        part = pl.ds(k * size, size)
        copies.append((
            pltpu.make_async_copy(turned.at[k], sides.at[k], sems.at[STEPS + k]),
            pltpu.make_async_copy(grads.at[part], held.at[part], sems.at[k]),
        ))
        for copy in copies[k]:
            copy.start()

    for copy in small:
        copy.wait()
    total = received[0:32, :]
    for r in range(1, 16):
        total = total + received[r * 32:(r + 1) * 32, :]
    for k in range(2):
        for h in range(2):
            where = index[k * 32:(k + 1) * 32, h * 128:(h + 1) * 128]
            value = lanes(total, jnp.maximum(where, 0))
            spread = (first, second)[h]
            spread[pl.ds(k, 32, stride=2), :] = jnp.where(where >= 0, value, 0.0)
    basis = (lh[...], ll[...])
    for q in range(4):
        part = (first, second)[q // 2][:, (q % 2) * 64:(q % 2) * 64 + 64]
        columns = dot3(split(part), basis)
        for f in range(4):
            piece = columns[:, f * 64:(f + 1) * 64]
            wide[q * 4 + f] = jnp.concatenate([piece, piece], axis=1)

    @pl.loop(0, CH // 2, unroll=4)
    def _(pair):
        row = pl.multiple_of(pair * BAND, BAND)
        factors = weights[pl.ds(row, BAND), :]
        value = wide[0] * factors[0:1]
        for f in range(1, BAND):
            value = value + wide[f] * factors[f:f + 1]
        rows[:, pl.ds(pl.multiple_of(pair * 128, 128), 128)] = value.astype(BF16)

    decoded = pltpu.make_async_copy(rows, update, sems.at[last + 6])
    decoded.start()
    for k in range(STEPS):
        for copy in copies[k]:
            copy.wait()
        part = slice(k * size, (k + 1) * size)
        for q in range(4):
            cols = slice(q * 256, (q + 1) * 256)
            out[:, cols] = (start if k == 0 else out)[:, cols] + dot(sides[k], held[part, cols])
    decoded.wait()


def vmem(n):
    return [pl.BlockSpec(memory_space=pltpu.VMEM)] * n


def sds(shape, dtype=F32):
    return jax.ShapeDtypeStruct(shape, dtype)


def call(kernel, shapes, *args, scalars=0, limit=40):
    scalar = [pl.BlockSpec(memory_space=pltpu.SMEM)] * scalars
    many = isinstance(shapes, tuple)
    return pl.pallas_call(
        kernel,
        out_shape=shapes,
        in_specs=scalar + vmem(len(args) - scalars),
        out_specs=tuple(vmem(len(shapes))) if many else vmem(1)[0],
        compiler_params=pltpu.CompilerParams(vmem_limit_bytes=limit << 20),
        name=kernel.__name__,
    )(*args)


def far(*args):
    return pl.pallas_call(
        far_kernel,
        out_shape=(sds((64, 256)), sds((512, 128))),
        in_specs=[pl.BlockSpec(memory_space=pltpu.SMEM)] + vmem(len(args) - 1),
        out_specs=(pl.BlockSpec(memory_space=pl.ANY), vmem(1)[0]),
        scratch_shapes=[pltpu.VMEM((64, 256), F32), pltpu.SemaphoreType.DMA((1,))],
        compiler_params=pltpu.CompilerParams(vmem_limit_bytes=40 << 20),
        name="far",
    )(*args)


def final(turned, grads, base, received, index, lh, ll):
    table = band_table().T.reshape(CH // 2, 2, BAND).transpose(0, 2, 1)
    weights = np.repeat(table, 64, axis=2).reshape(CH // 2 * BAND, 128).astype(np.float32)
    return pl.pallas_call(
        final_kernel,
        out_shape=(sds((ROWS, WIDTH)), sds((64, CH * CH), BF16)),
        in_specs=[pl.BlockSpec(memory_space=pl.ANY)] * 8,
        out_specs=(vmem(1)[0], pl.BlockSpec(memory_space=pl.ANY)),
        scratch_shapes=[
            pltpu.VMEM((STEPS, ROWS, TOKENS // STEPS), BF16), pltpu.VMEM((TOKENS, WIDTH), BF16),
            pltpu.VMEM((ROWS, WIDTH), F32),
            pltpu.VMEM((512, 128), F32), pltpu.VMEM((64, 256), I32), pltpu.VMEM((CH // 2 * BAND, 128), F32),
            pltpu.VMEM((64, 256), BF16), pltpu.VMEM((64, 256), BF16),
            pltpu.VMEM((64, 128), F32), pltpu.VMEM((64, 128), F32), pltpu.VMEM((BAND, 64, 128), F32),
            pltpu.VMEM((64, CH * CH), BF16), pltpu.SemaphoreType.DMA((2 * STEPS + 7,)),
        ],
        compiler_params=pltpu.CompilerParams(vmem_limit_bytes=56 << 20),
        cost_estimate=pl.CostEstimate(flops=2 * TOKENS * ROWS * WIDTH, bytes_accessed=14 << 20, transcendentals=0),
        name="final",
    )(turned, grads, base, received, index, weights, lh, ll)


def shard(z, x, c):
    return (z * 4 + x) * 2 + c


ALONG_X = [[shard(z, x, c) for x in range(4)] for z in range(4) for c in range(2)]
ALONG_Z = [[shard(z, x, c) for z in range(4)] for x in range(4) for c in range(2)]
OTHER_CORE = [(i, i ^ 1) for i in range(32)]


def exchange(copies, groups):
    return lax.all_to_all(copies, "shard", 0, 0, tiled=True, axis_index_groups=groups)


def body(activations, key_grads, momentum, freq_rows, freq_cols, dispatch):
    place = lax.axis_index("shard").astype(I32).reshape(1)
    lh, ll = split_np(block_basis())
    th, tl = lh.T.copy(), ll.T.copy()
    all_grads = lax.all_gather(key_grads, "shard", axis=0, tiled=True)

    band = call(project_kernel, sds((4 * SENT, 256), jnp.int16), key_grads, th, tl, limit=56)
    along_z = exchange(band, ALONG_Z)
    mask, col_index, row_pick, slot_row, slot_lane, index = call(
        tables_kernel,
        (sds((64, 256)), sds((8, 128), I32), sds((32, 128), I32), sds((32, 128), I32), sds((32, 128), I32),
         sds((64, 256), I32)),
        place, jnp.transpose(freq_rows, (1, 2, 0)), jnp.transpose(freq_cols, (1, 2, 0)), dispatch, scalars=1,
    )
    along_z, slot_row, after = lax.optimization_barrier((along_z, slot_row, jnp.asarray(lh)))
    own = exchange(call(repack_kernel, sds((4 * PACKED, 256), jnp.int16), along_z), ALONG_X)
    high, low, kept = call(
        prepare_kernel,
        (sds((2, 64, 2048), BF16), sds((2, 64, 2048), BF16), sds((64, 256))),
        activations, momentum, after, ll, th, tl,
    )
    own, kept = lax.optimization_barrier((own, kept))

    other = lax.ppermute(own, "shard", OTHER_CORE)
    near = call(near_kernel, sds((64, 256)), place, high, low, own, kept, scalars=1)
    coef, board = far(place, high, low, other, near, col_index, row_pick, slot_row, slot_lane)
    received = lax.all_to_all(board, ("rep", "shard"), 0, 0, tiled=True)
    turned, base = call(
        ready_kernel, (sds((STEPS, ROWS, TOKENS // STEPS), BF16), sds((ROWS, WIDTH))),
        activations, momentum, coef, mask, lh, ll, th, tl,
    )
    new_momentum, update = final(turned, all_grads, base, received, index, lh, ll)
    return (new_momentum, update)


def solution(mesh):
    in_specs = (
        P("rep", "shard"),
        P(("rep", "shard"), None),
        P(("rep", "shard"), None),
        P(),
        P(),
        P(),
    )
    out_specs = (P(("rep", "shard"), None), P("shard", None))
    return jax.shard_map(body, mesh=mesh, in_specs=in_specs, out_specs=out_specs, check_vma=False)
```

```python
import jax
import jax.numpy as jnp
import numpy as np
from jax import lax
from jax.experimental import pallas as pl
from jax.experimental.pallas import tpu as pltpu
from jax.sharding import PartitionSpec as P

CH = 64
K = 8
BAND = 16
ROWS = 256
WIDTH = 1024
TOKENS = 4096
STEPS = 4
LEVELS = 32000.0
SENT = 144
PACKED = 528
F32 = jnp.float32
BF16 = jnp.bfloat16
I32 = jnp.int32


def band_table():
    frequency = np.arange(BAND)[:, None]
    sample = np.arange(CH)[None, :]
    scales = np.where(frequency == 0, np.sqrt(1.0 / CH), np.sqrt(2.0 / CH))
    return scales * np.cos(np.pi * (2.0 * sample + 1.0) * frequency / (2.0 * CH))


def split_np(x):
    hi = x.astype(np.float32).astype(jnp.bfloat16)
    lo = (x - hi.astype(np.float64)).astype(np.float32).astype(jnp.bfloat16)
    return hi, lo


def block_basis():
    return np.kron(np.eye(4), band_table())


def split(x):
    hi = x.astype(BF16)
    return hi, (x - hi.astype(F32)).astype(BF16)


def dot(x, y):
    return lax.dot_general(x, y, (((1,), (0,)), ((), ())), preferred_element_type=F32)


def nt(x, y):
    return lax.dot_general(x, y, (((1,), (1,)), ((), ())), preferred_element_type=F32)


def dot3(x, y):
    (xh, xl), (yh, yl) = x, y
    return dot(xh, yh) + (dot(xh, yl) + dot(xl, yh))


def lanes(x, index):
    return jnp.take_along_axis(x, index, axis=1)


def iota(shape, axis):
    return lax.broadcasted_iota(I32, shape, axis)


def power(exponent):
    return jnp.exp2(exponent).astype(BF16).astype(F32)


def project_kernel(grads, th, tl, out):
    parts = []
    for q in range(4):
        part = grads[:, q * 256:(q + 1) * 256]
        parts.append(dot(part, th[...]) + dot(part, tl[...]))
    band = jnp.concatenate(parts, axis=1)
    top = jnp.maximum(jnp.max(jnp.abs(band), axis=1, keepdims=True), 1e-30)
    exponent = jnp.broadcast_to(jnp.ceil(jnp.log2(top)), (128, 128))
    code = jnp.floor(band * (power(-exponent[:, :1]) * LEVELS) + 0.5)
    scales = jnp.concatenate([exponent.T[:16]] * 2, axis=1)
    sent = jnp.concatenate([code, scales], axis=0).astype(I32).astype(jnp.int16)
    for k in range(4):
        out[k * SENT:(k + 1) * SENT, :] = sent


def tables_kernel(place, freq_rows, freq_cols, dispatch, mask, col_index, row_pick, slot_row, slot_lane, index):
    s = place[0]
    rows = freq_rows[...].reshape(128, 128).astype(F32).astype(BF16)
    cols = freq_cols[...].reshape(128, 128).astype(F32).astype(BF16)
    sub, lane = iota((8, 128), 0), iota((8, 128), 1)
    pick = jnp.where((lane == s * 4 + sub) & (sub < 4), 1.0, 0.0).astype(BF16)
    my_rows = nt(pick, rows).astype(I32)
    my_cols = nt(pick, cols).astype(I32)
    col_index[...] = my_cols + ((lane >> 3) & 7) * BAND
    for i in range(K):
        value = lanes(my_rows, (lane & 120) + i)
        for a in range(4):
            row_pick[a * K + i:a * K + i + 1, :] = value[a:a + 1]
    f1 = iota((BAND, 128), 0)
    for h in range(2):
        source = h * 64 + (lane >> 4) * K
        hit = jnp.zeros((8, 128), I32)
        for j in range(K):
            hit += jnp.where(lanes(my_cols, source + j) == (lane & 15), 1, 0)
        values = [lanes(my_rows, source + i) for i in range(K)]
        for a in range(4):
            found = jnp.zeros((BAND, 128), I32)
            for value in values:
                found += jnp.where(jnp.broadcast_to(value[a:a + 1], (BAND, 128)) == f1, 1, 0)
            both = found * jnp.broadcast_to(hit[a:a + 1], (BAND, 128))
            mask[a * BAND:(a + 1) * BAND, h * 128:(h + 1) * 128] = both.astype(F32)

    def doubled(x):
        return jnp.concatenate([x, x], axis=1)

    sub, lane = iota((32, 128), 0), iota((32, 128), 1)
    mine = jnp.broadcast_to(doubled(dispatch[pl.ds(s, 1), :]), (32, 128))
    slot = lanes(mine, sub * 2 + (lane >> 6))
    slot_row[...] = (slot >> 4) * K + ((lane >> 3) & 7)
    slot_lane[...] = (slot & 15) * K + (lane & 7)

    whole = doubled(dispatch[...])
    owned = [lanes(whole, jnp.zeros((32, 128), I32) + (s * 2 + k)) for k in range(2)]
    owned = jnp.concatenate(owned, axis=0)
    sub, lane = iota((64, 128), 0), iota((64, 128), 1)
    pick = jnp.where(lane == (sub & 31) * 4 + (owned >> 4), 1.0, 0.0).astype(BF16)
    own_rows = nt(pick, rows).astype(I32)
    own_cols = nt(pick, cols).astype(I32)
    first = (owned & 15) * K
    row_values = [lanes(own_rows, first + i) for i in range(K)]
    col_values = [lanes(own_cols, first + i) for i in range(K)]

    def at(values, frequency):
        seen, where = jnp.zeros((64, 128), I32), jnp.zeros((64, 128), I32)
        for i, value in enumerate(values):
            same = value == frequency
            seen += jnp.where(same, 1, 0)
            where += jnp.where(same, i, 0)
        return seen, where

    col_seen, col_at = at(col_values, lane & 15)
    start = (sub >> 5) * 64
    for h in range(2):
        row_seen, row_at = at(row_values, h * 8 + (lane >> 4))
        found = start + row_at * K + col_at
        index[:, h * 128:(h + 1) * 128] = jnp.where(row_seen * col_seen > 0, found, -1)


def prepare_kernel(inputs, momentum, lh, ll, th, tl, high, low, kept):
    both_basis = jnp.concatenate([lh[...], ll[...]], axis=0)
    for z in range(4):
        for x in range(4):
            for c in range(2):
                at = ((z * 4 + x) * 2 + c) * 128
                block = inputs[at:at + 128, :]
                both = nt(both_basis, block)
                part = split(both[:64] + both[64:])
                to = (x * 4 + z) * 128
                high[c, :, to:to + 128] = part[0]
                low[c, :, to:to + 128] = part[1]
    left, right = (lh[...], ll[...]), (th[...], tl[...])
    half = dot3(left, split(0.999 * momentum[...]))
    for q in range(4):
        kept[:, q * 64:(q + 1) * 64] = dot3(split(half[:, q * 256:(q + 1) * 256]), right)


def repack_kernel(along_z, out):
    row = iota((16, 256), 0)
    scales = jnp.zeros((16, 256), I32)
    for z in range(4):
        scales = jnp.where(row == z, along_z[z * SENT + 128:(z + 1) * SENT, :].astype(I32), scales)
    scales = scales.astype(jnp.int16)
    for x in range(4):
        for z in range(4):
            out[x * PACKED + z * 128:x * PACKED + (z + 1) * 128, :] = along_z[z * SENT:z * SENT + 128, :]
        out[x * PACKED + 512:(x + 1) * PACKED, :] = scales


def contract(high, low, side, source):
    total = jnp.zeros((64, 256), F32)
    for k in range(16):
        x, z = k // 4, k % 4
        at, to = x * PACKED + z * 128, k * 128
        xh, xl = split(source[at:at + 128, :].astype(I32).astype(F32))
        scale = power(source[x * PACKED + 512:(x + 1) * PACKED, :].astype(I32).astype(F32)[z:z + 1, :128]).astype(BF16)
        left = jnp.concatenate([high[side, :, to:to + 128], low[side, :, to:to + 128]], axis=0)
        left = left * jnp.broadcast_to(scale, (128, 128))
        both = dot(left, xh)
        total += both[:64] + (both[64:] + dot(left[:64], xl))
    return total * (1.0 / LEVELS)


def near_kernel(place, high, low, own, kept, out):
    out[...] = kept[...] + contract(high, low, place[0] & 1, own)


def select(low, high, col_index, row_pick, slot_row, slot_lane):
    lane = iota((BAND, 128), 1)
    picked = []
    for a in range(4):
        rows = slice(a * BAND, (a + 1) * BAND)
        index = jnp.broadcast_to(col_index[a:a + 1, :], (BAND, 128))
        cols = jnp.where(lane < 64, lanes(low[rows], index), lanes(high[rows], index))
        want = row_pick[a * K:(a + 1) * K, :]
        total = jnp.zeros((K, 128), F32)
        for f in range(BAND):
            total = jnp.where(want == f, jnp.broadcast_to(cols[f:f + 1], (K, 128)), total)
        picked.append(total)
    code, place = slot_row[...], slot_lane[...]
    board = jnp.zeros((32, 128), F32)
    for a in range(4):
        for i in range(K):
            row = jnp.broadcast_to(picked[a][i:i + 1], (32, 128))
            board = jnp.where(code == a * K + i, lanes(row, place), board)
    return board


def far_kernel(place, high, low, other, near, col_index, row_pick, slot_row, slot_lane, coef, sent, held, sem):
    total = near[...] + contract(high, low, 1 - (place[0] & 1), other)
    held[...] = total
    copy = pltpu.make_async_copy(held, coef, sem.at[0])
    copy.start()
    board = select(total[:, :128], total[:, 128:], col_index, row_pick, slot_row, slot_lane)
    for r in range(16):
        sent[r * 32:(r + 1) * 32, :] = board
    copy.wait()


def ready_kernel(inputs, momentum, coef, mask, lh, ll, th, tl, turned, base):
    size = TOKENS // STEPS
    for k in range(STEPS):
        turned[k] = inputs[k * size:(k + 1) * size, :].T
    left, right = (lh[...], ll[...]), (th[...], tl[...])
    back = dot3(right, split(coef[...] * mask[...]))
    for q in range(4):
        cols = slice(q * 256, (q + 1) * 256)
        base[:, cols] = 0.999 * momentum[:, cols] - dot3(split(back[:, q * 64:(q + 1) * 64]), left)


def final_kernel(turned, grads, base, *refs):
    sources, (out, update), (sides, held, start), refs = refs[:5], refs[5:7], refs[7:10], refs[10:]
    (received, index, weights, lh, ll), (first, second, wide, rows, sems) = refs[:5], refs[5:]
    size = TOKENS // STEPS
    last = 2 * STEPS
    small = [pltpu.make_async_copy(x, y, sems.at[last + 1 + k]) for k, (x, y) in enumerate(zip(sources, refs[:5]))]
    small.append(pltpu.make_async_copy(base, start, sems.at[last]))
    for copy in small:
        copy.start()
    copies = []
    for k in range(STEPS):
        part = pl.ds(k * size, size)
        copies.append((
            pltpu.make_async_copy(turned.at[k], sides.at[k], sems.at[STEPS + k]),
            pltpu.make_async_copy(grads.at[part], held.at[part], sems.at[k]),
        ))
        for copy in copies[k]:
            copy.start()

    for copy in small:
        copy.wait()
    total = received[0:32, :]
    for r in range(1, 16):
        total = total + received[r * 32:(r + 1) * 32, :]
    for k in range(2):
        for h in range(2):
            where = index[k * 32:(k + 1) * 32, h * 128:(h + 1) * 128]
            value = lanes(total, jnp.maximum(where, 0))
            spread = (first, second)[h]
            spread[pl.ds(k, 32, stride=2), :] = jnp.where(where >= 0, value, 0.0)
    basis = (lh[...], ll[...])
    for q in range(4):
        part = (first, second)[q // 2][:, (q % 2) * 64:(q % 2) * 64 + 64]
        columns = dot3(split(part), basis)
        for f in range(4):
            piece = columns[:, f * 64:(f + 1) * 64]
            wide[q * 4 + f] = jnp.concatenate([piece, piece], axis=1)

    @pl.loop(0, CH // 2, unroll=4)
    def _(pair):
        row = pl.multiple_of(pair * BAND, BAND)
        factors = weights[pl.ds(row, BAND), :]
        value = wide[0] * factors[0:1]
        for f in range(1, BAND):
            value = value + wide[f] * factors[f:f + 1]
        rows[:, pl.ds(pl.multiple_of(pair * 128, 128), 128)] = value.astype(BF16)

    decoded = pltpu.make_async_copy(rows, update, sems.at[last + 6])
    decoded.start()
    for k in range(STEPS):
        for copy in copies[k]:
            copy.wait()
        part = slice(k * size, (k + 1) * size)
        for q in range(4):
            cols = slice(q * 256, (q + 1) * 256)
            out[:, cols] = (start if k == 0 else out)[:, cols] + dot(sides[k], held[part, cols])
    decoded.wait()


def vmem(n):
    return [pl.BlockSpec(memory_space=pltpu.VMEM)] * n


def sds(shape, dtype=F32):
    return jax.ShapeDtypeStruct(shape, dtype)


def call(kernel, shapes, *args, scalars=0, limit=40):
    scalar = [pl.BlockSpec(memory_space=pltpu.SMEM)] * scalars
    many = isinstance(shapes, tuple)
    return pl.pallas_call(
        kernel,
        out_shape=shapes,
        in_specs=scalar + vmem(len(args) - scalars),
        out_specs=tuple(vmem(len(shapes))) if many else vmem(1)[0],
        compiler_params=pltpu.CompilerParams(vmem_limit_bytes=limit << 20),
        name=kernel.__name__,
    )(*args)


def far(*args):
    return pl.pallas_call(
        far_kernel,
        out_shape=(sds((64, 256)), sds((512, 128))),
        in_specs=[pl.BlockSpec(memory_space=pltpu.SMEM)] + vmem(len(args) - 1),
        out_specs=(pl.BlockSpec(memory_space=pl.ANY), vmem(1)[0]),
        scratch_shapes=[pltpu.VMEM((64, 256), F32), pltpu.SemaphoreType.DMA((1,))],
        compiler_params=pltpu.CompilerParams(vmem_limit_bytes=40 << 20),
        name="far",
    )(*args)


def final(turned, grads, base, received, index, lh, ll):
    table = band_table().T.reshape(CH // 2, 2, BAND).transpose(0, 2, 1)
    weights = np.repeat(table, 64, axis=2).reshape(CH // 2 * BAND, 128).astype(np.float32)
    return pl.pallas_call(
        final_kernel,
        out_shape=(sds((ROWS, WIDTH)), sds((64, CH * CH), BF16)),
        in_specs=[pl.BlockSpec(memory_space=pl.ANY)] * 8,
        out_specs=(vmem(1)[0], pl.BlockSpec(memory_space=pl.ANY)),
        scratch_shapes=[
            pltpu.VMEM((STEPS, ROWS, TOKENS // STEPS), BF16), pltpu.VMEM((TOKENS, WIDTH), BF16),
            pltpu.VMEM((ROWS, WIDTH), F32),
            pltpu.VMEM((512, 128), F32), pltpu.VMEM((64, 256), I32), pltpu.VMEM((CH // 2 * BAND, 128), F32),
            pltpu.VMEM((64, 256), BF16), pltpu.VMEM((64, 256), BF16),
            pltpu.VMEM((64, 128), F32), pltpu.VMEM((64, 128), F32), pltpu.VMEM((BAND, 64, 128), F32),
            pltpu.VMEM((64, CH * CH), BF16), pltpu.SemaphoreType.DMA((2 * STEPS + 7,)),
        ],
        compiler_params=pltpu.CompilerParams(vmem_limit_bytes=56 << 20),
        cost_estimate=pl.CostEstimate(flops=2 * TOKENS * ROWS * WIDTH, bytes_accessed=14 << 20, transcendentals=0),
        name="final",
    )(turned, grads, base, received, index, weights, lh, ll)


def shard(z, x, c):
    return (z * 4 + x) * 2 + c


ALONG_X = [[shard(z, x, c) for x in range(4)] for z in range(4) for c in range(2)]
ALONG_Z = [[shard(z, x, c) for z in range(4)] for x in range(4) for c in range(2)]
OTHER_CORE = [(i, i ^ 1) for i in range(32)]


def exchange(copies, groups):
    return lax.all_to_all(copies, "shard", 0, 0, tiled=True, axis_index_groups=groups)


def body(activations, key_grads, momentum, freq_rows, freq_cols, dispatch):
    place = lax.axis_index("shard").astype(I32).reshape(1)
    lh, ll = split_np(block_basis())
    th, tl = lh.T.copy(), ll.T.copy()
    all_grads = lax.all_gather(key_grads, "shard", axis=0, tiled=True)

    band = call(project_kernel, sds((4 * SENT, 256), jnp.int16), key_grads, th, tl, limit=56)
    along_z = exchange(band, ALONG_Z)
    mask, col_index, row_pick, slot_row, slot_lane, index = call(
        tables_kernel,
        (sds((64, 256)), sds((8, 128), I32), sds((32, 128), I32), sds((32, 128), I32), sds((32, 128), I32),
         sds((64, 256), I32)),
        place, jnp.transpose(freq_rows, (1, 2, 0)), jnp.transpose(freq_cols, (1, 2, 0)), dispatch, scalars=1,
    )
    along_z, slot_row, after = lax.optimization_barrier((along_z, slot_row, jnp.asarray(lh)))
    own = exchange(call(repack_kernel, sds((4 * PACKED, 256), jnp.int16), along_z), ALONG_X)
    high, low, kept = call(
        prepare_kernel,
        (sds((2, 64, 2048), BF16), sds((2, 64, 2048), BF16), sds((64, 256))),
        activations, momentum, after, ll, th, tl,
    )
    own, kept = lax.optimization_barrier((own, kept))

    other = lax.ppermute(own, "shard", OTHER_CORE)
    near = call(near_kernel, sds((64, 256)), place, high, low, own, kept, scalars=1)
    coef, board = far(place, high, low, other, near, col_index, row_pick, slot_row, slot_lane)
    received = lax.all_to_all(board, ("rep", "shard"), 0, 0, tiled=True)
    turned, base = call(
        ready_kernel, (sds((STEPS, ROWS, TOKENS // STEPS), BF16), sds((ROWS, WIDTH))),
        activations, momentum, coef, mask, lh, ll, th, tl,
    )
    new_momentum, update = final(turned, all_grads, base, received, index, lh, ll)
    return (new_momentum, update)


def solution(mesh):
    in_specs = (
        P("rep", "shard"),
        P(("rep", "shard"), None),
        P(("rep", "shard"), None),
        P(),
        P(),
        P(),
    )
    out_specs = (P(("rep", "shard"), None), P("shard", None))
    return jax.shard_map(body, mesh=mesh, in_specs=in_specs, out_specs=out_specs, check_vma=False)
```
